128 devices in a mesh: gx: 8 (over z_hi, x), gy: 16 (over y, z_lo, core).
Axes of the slice: x: 4, y: 4, z: 4 (z_hi: 2, z_lo: 2; z = z_hi * 2 + z_lo), core: 2. Of those that a mesh axis runs over, the one named last changes fastest.
Arguments:
- inputs: bfloat16 [1024, 8192], P('gx', 'gy'), may hold values from -6 to 6
- out_grad: bfloat16 [1024, 8192], P('gx', 'gy'), may hold values from -1.1953125 to 1.1953125
- pre_act: bfloat16 [1024, 32768], P('gy', 'gx'), may hold values from -6 to 6
- w_in: bfloat16 [8192, 32768], P('gy', 'gx'), may hold values from -0.0625 to 0.0625
- w_out: bfloat16 [32768, 8192], P('gx', 'gy'), may hold values from -0.03125 to 0.03125
- counts: int32 [8], replicated, may hold values from 1 to 128, 640 in all
Outputs:
- in_grad: bfloat16 [1024, 8192], P('gx', 'gy')
- w_in_grad: bfloat16 [8192, 32768], P('gy', 'gx')
- w_out_grad: bfloat16 [32768, 8192], P('gx', 'gy')
The draws below stay inside these ranges and needn't reach their ends.
Inputs may be any that keep to these rules, and one draw needn't show every extreme that they name: In batch shard s (token slots s * 128 to (s + 1) * 128 - 1) the first counts[s] slots are live and the rest are padding; the counts add up to exactly 640, and at least one shard is full.
All inputs are finite; a program needn't handle non-finite values.
Results may differ from the reference program's by a relative error of at most 0.0051.
Values may be sent and summed in bfloat16 or wider, within the bound.
A program may use at most 128 MiB of HBM per device.

```python
import math
import jax
import jax.numpy as jnp
import numpy as np

D = 8192
FF = 32768
TOK_SHARD = 128
TOKENS = 1024
LIVE = 640
N_GX = 8


def shard_levels(own_key, extent, split, least, high):
    loudness = 1.0
    for axis_at, blocks in split:
        draws = jax.random.uniform(jax.random.fold_in(jax.random.fold_in(own_key, 6), axis_at), (blocks,), jnp.float32, least / len(split), high / len(split))
        loudness = loudness * jnp.repeat(jnp.exp(draws), extent[axis_at] // blocks).reshape((-1,) + (1,) * (len(extent) - 1 - axis_at))
    return loudness


def profile(count, total, most, lean):
    portions = [(1 << 20) // math.isqrt(standing ** lean) + 1 for standing in range(2, count + 1)]
    spare, given = total - most - (count - 1), [1] * (count - 1)
    while spare > 0:
        movable = [i for i in range(count - 1) if given[i] < most]
        pool, budget = sum([portions[i] for i in movable]), spare
        for i in movable:
            extra = min(most - given[i], max(1, budget * portions[i] // pool), spare)
            given[i] = given[i] + extra
            spare = spare - extra
    return np.array([most] + given)


def uneven(stream_key, count, total, bound, skew):
    if count == 2:
        one = jax.random.randint(stream_key, (), max(1, total - bound), min(bound, total - 1) + 1)
        return jnp.stack([one, total - one])
    sizes = jnp.asarray(profile(count, total, bound, skew), jnp.int32)
    couples = (count - 1) // 2
    giver, taker = sizes[1:1 + 2 * couples:2], sizes[2:2 + 2 * couples:2]
    margin = jnp.minimum(giver - 1, bound - taker)
    moved = jax.random.randint(jax.random.fold_in(stream_key, 1), (couples,), 0, 1 << 20) % (margin + 1)
    sizes = sizes.at[1:1 + 2 * couples:2].set(giver - moved).at[2:2 + 2 * couples:2].set(taker + moved)
    return sizes[jax.random.permutation(jax.random.fold_in(stream_key, 2), count)]


def gaussian(key, shape, scale, most, shards=(), held_as=jnp.bfloat16):
    result = scale * jax.random.normal(key, shape, jnp.float32)
    if shards:
        result = result * shard_levels(key, shape, shards, -0.22, 0.18)
    return jnp.clip(result, -most, most).astype(held_as)


def setup_inputs(seed: int = 0) -> dict:
    splits = jax.random.split(jax.random.key(seed), 7)
    inputs = gaussian(splits[0], (TOKENS, D), 1.0, 6.0, ((0, 8), (1, 16)))
    out_grad = gaussian(splits[1], (TOKENS, D), 0.2, 1.1953125, ((0, 8), (1, 16)))
    pre_act = gaussian(splits[2], (TOKENS, FF), 1.0, 6.0, ((0, 16), (1, 8)))
    w_in = gaussian(splits[3], (D, FF), D ** -0.5, 0.0625, ((0, 16), (1, 8)))
    w_out = gaussian(splits[4], (FF, D), FF ** -0.5, 0.03125, ((0, 8), (1, 16)))
    counts = uneven(splits[5], N_GX, LIVE, TOK_SHARD, 2).astype(jnp.int32)
    return {"inputs": inputs, "out_grad": out_grad, "pre_act": pre_act, "w_in": w_in, "w_out": w_out, "counts": counts}


gelu_scale = math.sqrt(2.0 / math.pi)
cubic_coef = 0.044715

def gelu_parts(pre):
    inner_arg = gelu_scale * (pre + cubic_coef * pre * pre * pre)
    tangent = jnp.tanh(inner_arg)
    value = 0.5 * pre * (1.0 + tangent)
    slope = 0.5 * (1.0 + tangent) + 0.5 * pre * (1.0 - tangent * tangent) * gelu_scale * (1.0 + 3.0 * cubic_coef * pre * pre)
    return (value, slope)

def reference(inputs, out_grad, pre_act, w_in, w_out, counts):
    positions = jnp.arange(TOKENS, dtype=jnp.int32)
    owner_shard = (positions // TOK_SHARD).astype(jnp.int32)
    is_live = positions % TOK_SHARD < counts[owner_shard]
    masked_grad = jnp.where(is_live[:, None], out_grad, jnp.zeros_like(out_grad))
    value, slope = gelu_parts(pre_act.astype(jnp.float32))
    activation = value.astype(jnp.bfloat16)
    w_out_grad = jnp.dot(activation.T, masked_grad, preferred_element_type=jnp.float32).astype(jnp.bfloat16)
    hidden_sum = jnp.dot(masked_grad, w_out.T, preferred_element_type=jnp.float32)
    hidden_grad = (hidden_sum * slope).astype(jnp.bfloat16)
    w_in_grad = jnp.dot(inputs.T, hidden_grad, preferred_element_type=jnp.float32).astype(jnp.bfloat16)
    in_grad = jnp.dot(hidden_grad, w_in.T, preferred_element_type=jnp.float32).astype(jnp.bfloat16)
    return (in_grad, w_in_grad, w_out_grad)
```

```python
import math

import jax
import jax.numpy as jnp
from jax import lax
from jax.sharding import PartitionSpec as P

LIVE = 640
gelu_scale = math.sqrt(2.0 / math.pi)
cubic_coef = 0.044715


def gelu_parts(pre):
    tangent = jnp.tanh(gelu_scale * (pre + cubic_coef * pre * pre * pre))
    value = 0.5 * pre * (1.0 + tangent)
    slope = 0.5 * (1.0 + tangent) + 0.5 * pre * (1.0 - tangent * tangent) * gelu_scale * (
        1.0 + 3.0 * cubic_coef * pre * pre
    )
    return value, slope


def token_sum(left, right):
    return lax.dot_general(
        left, right, (((0,), (0,)), ((), ())), preferred_element_type=jnp.float32
    )


def contract_last(left, right):
    return lax.dot_general(
        left, right, (((1,), (1,)), ((), ())), preferred_element_type=jnp.float32
    )


def pick_matrix(counts, shard_rows, all_rows, shards):
    token = jnp.arange(all_rows, dtype=jnp.int32)
    shard = jnp.arange(shards, dtype=jnp.int32)
    starts = jnp.sum(jnp.where(shard[None, :] < shard[:, None], counts[None, :], 0), axis=1)
    owner = token // shard_rows
    one_hot = owner[:, None] == jnp.arange(shards, dtype=jnp.int32)[None, :]
    own_count = jnp.sum(jnp.where(one_hot, counts[None, :], 0), axis=1)
    own_start = jnp.sum(jnp.where(one_hot, starts[None, :], 0), axis=1)
    slot = token % shard_rows
    place = jnp.where(slot < own_count, own_start + slot, -1)
    return (place[None, :] == jnp.arange(LIVE, dtype=jnp.int32)[:, None]).astype(jnp.bfloat16)


def body(inputs, out_grad, pre_act, w_in, w_out, counts):
    shard_rows = inputs.shape[0]
    shards = lax.axis_size("gx")
    all_rows = shard_rows * shards
    pick = pick_matrix(counts, shard_rows, all_rows, shards)

    def compact(whole):
        return jnp.dot(pick, whole, preferred_element_type=jnp.float32).astype(whole.dtype)

    live_dy = compact(lax.all_gather(out_grad, "gx", axis=0, tiled=True))
    live_x = compact(lax.all_gather(inputs, "gx", axis=0, tiled=True))
    my_pre = lax.all_to_all(pre_act, "gy", split_axis=1, concat_axis=0, tiled=True)
    value, slope = gelu_parts(compact(my_pre).astype(jnp.float32))
    activation = lax.all_gather(value.astype(jnp.bfloat16), "gy", axis=1, tiled=True)
    hidden = lax.psum_scatter(
        contract_last(live_dy, w_out), "gy", scatter_dimension=1, tiled=True
    )
    hidden_grad = lax.all_gather(
        (hidden * slope).astype(jnp.bfloat16), "gy", axis=1, tiled=True
    )
    w_out_grad = token_sum(activation, live_dy)
    w_in_grad = token_sum(live_x, hidden_grad)
    part = contract_last(hidden_grad, w_in)
    spread = lax.dot_general(
        pick, part.astype(jnp.bfloat16), (((0,), (0,)), ((), ())), preferred_element_type=jnp.float32
    )
    in_part = lax.psum_scatter(spread, "gx", scatter_dimension=0, tiled=True)
    return (
        in_part.astype(jnp.bfloat16),
        w_in_grad.astype(jnp.bfloat16),
        w_out_grad.astype(jnp.bfloat16),
    )


def solution(mesh):
    return jax.shard_map(
        body,
        mesh=mesh,
        in_specs=(P("gx", "gy"), P("gx", "gy"), P("gy", "gx"), P("gy", "gx"), P("gx", "gy"), P()),
        out_specs=(P("gx", "gy"), P("gy", "gx"), P("gx", "gy")),
        check_vma=False,
    )
```

```python
import math

import jax
import jax.numpy as jnp
from jax import lax
from jax.experimental import pallas as pl
from jax.experimental.pallas import tpu as pltpu
from jax.sharding import PartitionSpec as P

LIVE = 640
SHARDS = 8
ROWS = 128
FEAT = 512
PIECES = 16
UNITS = 256
HA = 128
HB = UNITS - HA
MESH = pl.DeviceIdType.MESH
BF16, F32 = jnp.bfloat16, jnp.float32

gelu_scale = math.sqrt(2.0 / math.pi)
cubic_coef = 0.044715


def gelu_parts(pre):
    tangent = jnp.tanh(gelu_scale * (pre + cubic_coef * pre * pre * pre))
    value = 0.5 * pre * (1.0 + tangent)
    slope = 0.5 * (1.0 + tangent) + 0.5 * pre * (1.0 - tangent * tangent) * gelu_scale * (
        1.0 + 3.0 * cubic_coef * pre * pre
    )
    return value, slope


def dot(left, right, left_dim, right_dim):
    return lax.dot_general(
        left, right, (((left_dim,), (right_dim,)), ((), ())), preferred_element_type=F32
    )


def kernel(
    counts, x_ref, dy_ref, pre_ref, w_in_ref, w_out_ref,
    in_out, wi_out, wo_out,
    pt, dyg, xg, preg, dyt, dys, xt, wo_own, wo_sib, wi, act, hg, slope,
    held, part, rz_a, rz_b, ry_a, ry_b, acc, accb, in_send, in_recv, wig, wog,
    send_sem, recv_sem, local_sem,
):
    gx, gy = lax.axis_index("gx"), lax.axis_index("gy")
    x, zh = gx % 4, gx // 4
    core, z, y = gy % 2, (gy // 2) % 2, gy // 4

    def on_gy(dy, dz, dc=0):
        return ((y + dy) % 4) * 4 + ((z + dz) % 2) * 2 + (core + dc) % 2

    def on_gx(dx, dzh):
        return ((zh + dzh) % 2) * 4 + (x + dx) % 4

    YP, YM, Z, C = (gx, on_gy(1, 0)), (gx, on_gy(3, 0)), (gx, on_gy(0, 1)), (gx, on_gy(0, 0, 1))
    XP, XM, ZH = (on_gx(1, 0), gy), (on_gx(3, 0), gy), (on_gx(0, 1), gy)

    count = [0, 0]
    sent, stored = [], []

    def send(src, dst, device):
        k = count[0]
        count[0] += 1
        copy = pltpu.make_async_remote_copy(
            src_ref=src, dst_ref=dst, send_sem=send_sem.at[k], recv_sem=recv_sem.at[k],
            device_id=device, device_id_type=MESH,
        )
        copy.start()
        sent.append(copy)
        return copy

    def local(src, dst):
        k = count[1]
        count[1] += 1
        copy = pltpu.make_async_copy(src, dst, local_sem.at[k])
        copy.start()
        return copy

    own_pre = local(pre_ref.at[:, pl.ds(pl.multiple_of(gy * UNITS, UNITS), UNITS)], preg.at[gy])
    load_wo = local(w_out_ref.at[:, core], wo_own)
    load_wi = local(w_in_ref, wi)
    barrier = pltpu.get_barrier_semaphore()
    for d in range(1, PIECES):
        pl.semaphore_signal(barrier, inc=1, device_id=(gx, (gy + d) % PIECES), device_id_type=MESH)
    for d in range(1, SHARDS):
        pl.semaphore_signal(barrier, inc=1, device_id=((gx + d) % SHARDS, gy), device_id_type=MESH)

    start = jnp.int32(0)
    for s in range(SHARDS):
        number = counts[s]

        def fill(i, carry, s=s, start=start, number=number):
            slot = lax.broadcasted_iota(jnp.int32, (16, LIVE), 0) + i * 16
            column = lax.broadcasted_iota(jnp.int32, (16, LIVE), 1)
            hit = (column == slot + start) & (slot < number)
            pt[pl.ds(pl.multiple_of(s * ROWS + i * 16, 16), 16), :] = jnp.where(hit, 1.0, 0.0).astype(BF16)
            return carry

        lax.fori_loop(0, ROWS // 16, fill, 0)
        start = start + number
    dyg[gx] = dy_ref[...]
    xg[gx] = x_ref[...]
    pl.semaphore_wait(barrier, PIECES - 1 + SHARDS - 1)

    lo, hi = pl.ds(0, ROWS // 2), pl.ds(ROWS // 2, ROWS // 2)

    def ring_start(src, buf):
        return send(src, buf.at[gx], ZH), send(src, buf.at[gx], XP), send(src, buf.at[gx], XM)

    def ring_relay(buf, first):
        def pass_on(dzh, to_right, to_left):
            to_right.wait_recv()
            came = on_gx(3, dzh)
            a = send(buf.at[came, lo], buf.at[came, lo], XP)
            to_left.wait_recv()
            came = on_gx(1, dzh)
            b = send(buf.at[came, hi], buf.at[came, hi], XM)
            return [a, b]

        across, right, left = first
        across.wait_recv()
        other = on_gx(0, 1)
        right2 = send(buf.at[other], buf.at[other], XP)
        left2 = send(buf.at[other], buf.at[other], XM)
        return pass_on(0, right, left) + pass_on(1, right2, left2)

    dy_first = ring_start(dy_ref, dyg)
    swap_wo = send(w_out_ref.at[:, 1 - core], wo_sib, C)
    pre_copies = []
    for d in range(1, PIECES):
        to = (gy + d) % PIECES
        columns = pl.ds(pl.multiple_of(to * UNITS, UNITS), UNITS)
        pre_copies.append(send(pre_ref.at[:, columns], preg.at[gy], (gx, to)))
    dy_last = ring_relay(dyg, dy_first)
    x_first = ring_start(x_ref, xg)

    def compact(buf, width):
        whole = buf[...].reshape(SHARDS * ROWS, width)
        return dot(whole, pt[...], 0, 0)

    for copy in dy_last:
        copy.wait_recv()
    dyt[...] = compact(dyg, FEAT).astype(BF16)
    swap_dy = send(dyt, dys, C)
    load_wo.wait()
    swap_wo.wait_recv()

    rows_a, rows_b = pl.ds(0, HA), pl.ds(HA, HB)
    QA, QB = HA // 2, HB // 2
    a0, a1, b0, b1 = pl.ds(0, QA), pl.ds(QA, QA), pl.ds(HA, QB), pl.ds(HA + QB, QB)
    ring = {}

    def ring_send(key, dy, dz, q0, q1, land):
        if dy == 2:
            ring[key, "relay+"] = send(part.at[dy, dz, q0], land.at[0], YP)
            ring[key, "relay-"] = send(part.at[dy, dz, q1], land.at[1], YM)
        if dy == 1:
            ring[key, "direct+"] = send(part.at[dy, dz, q1], land.at[2], YP)
        if dy == 3:
            ring[key, "direct-"] = send(part.at[dy, dz, q0], land.at[3], YM)

    def ring_pass(key, dz, q0, q1, land):
        ring[key, "relay+"].wait_recv()
        part[1, dz, q0, :] = (held[1, dz, q0, :] + land[0].astype(F32)).astype(BF16)
        ring[key, "last+"] = send(part.at[1, dz, q0], land.at[4], YP)
        ring[key, "relay-"].wait_recv()
        part[3, dz, q1, :] = (held[3, dz, q1, :] + land[1].astype(F32)).astype(BF16)
        ring[key, "last-"] = send(part.at[3, dz, q1], land.at[5], YM)

    def ring_total(key, dz, q0, q1, land):
        ring[key, "direct-"].wait_recv()
        ring[key, "last+"].wait_recv()
        total0 = held[0, dz, q0, :] + land[3].astype(F32) + land[4].astype(F32)
        ring[key, "direct+"].wait_recv()
        ring[key, "last-"].wait_recv()
        total1 = held[0, dz, q1, :] + land[2].astype(F32) + land[5].astype(F32)
        return total0, total1

    swap_dy.wait_recv()
    z_copies = {}
    for dy, dz in ((2, 1), (2, 0), (1, 1), (3, 1), (0, 1), (1, 0), (3, 0), (0, 0)):
        chip = ((y + dy) % 4) * 2 + (z + dz) % 2
        total = dot(wo_own[chip], dyt[...], 1, 0) + dot(wo_sib[chip], dys[...], 1, 0)
        held[dy, dz] = total
        part[dy, dz] = total.astype(BF16)
        ring_send(("a", dz), dy, dz, a0, a1, ry_a.at[dz])
        if dz == 1:
            z_copies[dy] = send(part.at[dy, dz, rows_b], rz_b.at[dy], Z)

    own_pre.wait()
    for copy in pre_copies:
        copy.wait_recv()
    slope[...] = dot(preg[...].reshape(SHARDS * ROWS, UNITS), pt[...], 0, 0)

    def gelu(i, carry):
        rows = pl.ds(pl.multiple_of(i * 16, 16), 16)
        value, tilt = gelu_parts(slope[rows, :])
        act[gy, rows, :] = value.astype(BF16)
        slope[rows, :] = tilt
        return carry

    lax.fori_loop(0, UNITS // 16, gelu, 0)

    for dz in (1, 0):
        ring_pass(("a", dz), dz, a0, a1, ry_a.at[dz])
    x_last = ring_relay(xg, x_first)
    for dy in (2, 1, 3, 0):
        z_copies[dy].wait_recv()
        total = held[dy, 0, rows_b, :] + rz_b[dy].astype(F32)
        held[dy, 0, rows_b, :] = total
        part[dy, 0, rows_b, :] = total.astype(BF16)
        ring_send("b", dy, 0, b0, b1, ry_b)
        if dy == 3:
            ring_pass("b", 0, b0, b1, ry_b)
    total0, total1 = ring_total(("a", 1), 1, a0, a1, ry_a.at[1])
    part[0, 1, a0, :] = total0.astype(BF16)
    part[0, 1, a1, :] = total1.astype(BF16)
    z_last = send(part.at[0, 1, rows_a], rz_a, Z)

    def gather_a(buf):
        own = buf.at[gy, rows_a]
        return {"z": send(own, own, Z), "+": send(own, own, YP), "-": send(own, own, YM), "c": send(own, own, C)}

    def gather_b(buf):
        own = buf.at[gy, rows_b]
        return {"+": send(own, own, YP), "-": send(own, own, YM), "z": send(own, own, Z), "c": send(own, own, C)}

    def gather_rest(buf, fa, fb, use):
        sib = {(0, 0): [fa["c"], fb["c"]]}

        def fwd(dy, dz, rows, device):
            piece = buf.at[on_gy(dy, dz), rows]
            return send(piece, piece, device)

        def to_sibling(dy, dz, rows):
            sib.setdefault((dy, dz), []).append(fwd(dy, dz, rows, C))

        def done(dy, dz):
            for copy in sib[dy, dz]:
                copy.wait_recv()
            use(((y + dy) % 4) * 2 + (z + dz) % 2)

        fa["z"].wait_recv()
        plus = fwd(0, 1, rows_a, YP)
        minus = fwd(0, 1, rows_a, YM)
        to_sibling(0, 1, rows_a)
        fa["+"].wait_recv()
        a20p = fwd(3, 0, a0, YP)
        to_sibling(3, 0, rows_a)
        fa["-"].wait_recv()
        a20m = fwd(1, 0, a1, YM)
        to_sibling(1, 0, rows_a)
        fb["+"].wait_recv()
        b20p = fwd(3, 0, b0, YP)
        zm = fwd(3, 0, rows_b, Z)
        to_sibling(3, 0, rows_b)
        fb["-"].wait_recv()
        b20m = fwd(1, 0, b1, YM)
        zp = fwd(1, 0, rows_b, Z)
        to_sibling(1, 0, rows_b)
        done(0, 0)
        plus.wait_recv()
        a21p = fwd(3, 1, a0, YP)
        to_sibling(3, 1, rows_a)
        minus.wait_recv()
        a21m = fwd(1, 1, a1, YM)
        to_sibling(1, 1, rows_a)
        a20p.wait_recv()
        a20m.wait_recv()
        to_sibling(2, 0, rows_a)
        b20p.wait_recv()
        b20m.wait_recv()
        z2 = fwd(2, 0, rows_b, Z)
        to_sibling(2, 0, rows_b)
        fb["z"].wait_recv()
        to_sibling(0, 1, rows_b)
        done(3, 0)
        done(1, 0)
        zm.wait_recv()
        to_sibling(3, 1, rows_b)
        done(0, 1)
        a21p.wait_recv()
        a21m.wait_recv()
        to_sibling(2, 1, rows_a)
        zp.wait_recv()
        to_sibling(1, 1, rows_b)
        done(2, 0)
        done(3, 1)
        z2.wait_recv()
        to_sibling(2, 1, rows_b)
        done(1, 1)
        done(2, 1)

    act_a = gather_a(act)
    act_b = gather_b(act)

    total0, total1 = ring_total("b", 0, b0, b1, ry_b)
    hg[gy, b0, :] = (total0 * slope[b0, :]).astype(BF16)
    hg[gy, b1, :] = (total1 * slope[b1, :]).astype(BF16)
    hg_b = gather_b(hg)
    total0, total1 = ring_total(("a", 0), 0, a0, a1, ry_a.at[0])
    z_last.wait_recv()
    hg[gy, a0, :] = ((total0 + rz_a[a0, :].astype(F32)) * slope[a0, :]).astype(BF16)
    hg[gy, a1, :] = ((total1 + rz_a[a1, :].astype(F32)) * slope[a1, :]).astype(BF16)
    hg_a = gather_a(hg)

    for copy in x_last:
        copy.wait_recv()
    xt[...] = compact(xg, FEAT).astype(BF16)
    load_wi.wait()
    acc[...] = jnp.zeros_like(acc)

    def use_hg(chip):
        k = len(stored)
        pair = pl.ds(chip * 2, 2)
        columns = pl.ds(pl.multiple_of(chip * 2 * UNITS, 2 * UNITS), 2 * UNITS)

        def tile(i, carry):
            rows = pl.ds(pl.multiple_of(i * 128, 128), 128)
            block = hg[pair].reshape(2 * UNITS, LIVE)
            acc[rows, :] += dot(wi[rows, columns], block, 1, 0)
            wig[k, rows, :] = dot(xt[rows, :], block, 1, 1).astype(BF16)
            return carry

        lax.fori_loop(0, FEAT // 128, tile, 0)
        stored.append(local(wig.at[k], wi_out.at[:, columns]))

    gather_rest(hg, hg_a, hg_b, use_hg)

    accb[...] = acc[...].astype(BF16)
    in_copies = []
    for d in range(1, SHARDS):
        to = (gx + d) % SHARDS
        rows = pl.ds(pl.multiple_of(to * ROWS, ROWS), ROWS)
        in_send[d - 1] = dot(pt[rows, :], accb[...], 1, 1).astype(BF16)
        in_copies.append(send(in_send.at[d - 1], in_recv.at[d - 1], (to, gy)))

    def use_act(chip):
        k = len(stored) - 8
        pair = pl.ds(chip * 2, 2)

        def tile(i, carry):
            rows = pl.ds(pl.multiple_of(i * 128, 128), 128)
            block = act[chip * 2 + i // 2, pl.ds(pl.multiple_of((i % 2) * 128, 128), 128), :]
            wog[k, rows, :] = dot(block, dyt[...], 1, 1).astype(BF16)
            return carry

        lax.fori_loop(0, 2 * UNITS // 128, tile, 0)
        stored.append(
            local(wog.at[k], wo_out.at[pl.ds(pl.multiple_of(chip * 2 * UNITS, 2 * UNITS), 2 * UNITS)])
        )

    gather_rest(act, act_a, act_b, use_act)

    total = dot(pt[pl.ds(pl.multiple_of(gx * ROWS, ROWS), ROWS), :], accb[...], 1, 1)
    for k, copy in enumerate(in_copies):
        copy.wait_recv()
        total = total + in_recv[k].astype(F32)
    in_out[...] = total.astype(BF16)
    for copy in stored:
        copy.wait()
    for copy in sent:
        copy.wait_send()


def body(inputs, out_grad, pre_act, w_in, w_out, counts):
    vmem = pl.BlockSpec(memory_space=pltpu.VMEM)
    anywhere = pl.BlockSpec(memory_space=pl.ANY)
    qa, qb = HA // 2, HB // 2
    flops = 2 * 4 * LIVE * FEAT * UNITS * PIECES
    return pl.pallas_call(
        kernel,
        out_shape=(
            jax.ShapeDtypeStruct((ROWS, FEAT), BF16),
            jax.ShapeDtypeStruct((FEAT, PIECES * UNITS), BF16),
            jax.ShapeDtypeStruct((PIECES * UNITS, FEAT), BF16),
        ),
        in_specs=[pl.BlockSpec(memory_space=pltpu.SMEM), vmem, vmem, anywhere, anywhere, anywhere],
        out_specs=(vmem, anywhere, anywhere),
        scratch_shapes=[
            pltpu.VMEM((SHARDS * ROWS, LIVE), BF16),
            pltpu.VMEM((SHARDS, ROWS, FEAT), BF16),
            pltpu.VMEM((SHARDS, ROWS, FEAT), BF16),
            pltpu.VMEM((PIECES, SHARDS * ROWS // PIECES, UNITS), BF16),
            pltpu.VMEM((FEAT, LIVE), BF16),
            pltpu.VMEM((FEAT, LIVE), BF16),
            pltpu.VMEM((FEAT, LIVE), BF16),
            pltpu.VMEM((8, UNITS, FEAT), BF16),
            pltpu.VMEM((8, UNITS, FEAT), BF16),
            pltpu.VMEM((FEAT, PIECES * UNITS), BF16),
            pltpu.VMEM((PIECES, UNITS, LIVE), BF16),
            pltpu.VMEM((PIECES, UNITS, LIVE), BF16),
            pltpu.VMEM((UNITS, LIVE), F32),
            pltpu.VMEM((4, 2, UNITS, LIVE), F32),
            pltpu.VMEM((4, 2, UNITS, LIVE), BF16),
            pltpu.VMEM((HA, LIVE), BF16),
            pltpu.VMEM((4, HB, LIVE), BF16),
            pltpu.VMEM((2, 6, qa, LIVE), BF16),
            pltpu.VMEM((6, qb, LIVE), BF16),
            pltpu.VMEM((FEAT, LIVE), F32),
            pltpu.VMEM((FEAT, LIVE), BF16),
            pltpu.VMEM((SHARDS - 1, ROWS, FEAT), BF16),
            pltpu.VMEM((SHARDS - 1, ROWS, FEAT), BF16),
            pltpu.VMEM((8, FEAT, 2 * UNITS), BF16),
            pltpu.VMEM((8, 2 * UNITS, FEAT), BF16),
            pltpu.SemaphoreType.DMA((144,)),
            pltpu.SemaphoreType.DMA((144,)),
            pltpu.SemaphoreType.DMA((20,)),
        ],
        compiler_params=pltpu.CompilerParams(
            collective_id=0, has_side_effects=True, vmem_limit_bytes=60 * 1024 * 1024
        ),
        cost_estimate=pl.CostEstimate(flops=flops, bytes_accessed=16 << 20, transcendentals=UNITS * LIVE),
        name="ffn_backward",
    )(counts, inputs, out_grad, pre_act, w_in, w_out.reshape(8, 2, UNITS, FEAT))


def solution(mesh):
    return jax.shard_map(
        body,
        mesh=mesh,
        in_specs=(P("gx", "gy"), P("gx", "gy"), P("gy", "gx"), P("gy", "gx"), P("gx", "gy"), P()),
        out_specs=(P("gx", "gy"), P("gy", "gx"), P("gx", "gy")),
        check_vma=False,
    )
```

```python
import math

import jax
import jax.numpy as jnp
from jax import lax
from jax.experimental import pallas as pl
from jax.experimental.pallas import tpu as pltpu
from jax.sharding import PartitionSpec as P

LIVE = 640
SHARDS = 8
ROWS = 128
FEAT = 512
PIECES = 16
UNITS = 256
HA = 160
HACT = 192
HB = UNITS - HA
MESH = pl.DeviceIdType.MESH
BF16, F32 = jnp.bfloat16, jnp.float32

gelu_scale = math.sqrt(2.0 / math.pi)
cubic_coef = 0.044715


def gelu_parts(pre):
    tangent = jnp.tanh(gelu_scale * (pre + cubic_coef * pre * pre * pre))
    value = 0.5 * pre * (1.0 + tangent)
    slope = 0.5 * (1.0 + tangent) + 0.5 * pre * (1.0 - tangent * tangent) * gelu_scale * (
        1.0 + 3.0 * cubic_coef * pre * pre
    )
    return value, slope


def dot(left, right, left_dim, right_dim):
    return lax.dot_general(
        left, right, (((left_dim,), (right_dim,)), ((), ())), preferred_element_type=F32
    )


def kernel(
    counts, x_ref, dy_ref, pre_ref, w_in_ref, w_out_ref,
    in_out, wi_out, wo_out,
    pt, dyg, xg, preg, dyt, dys, xt, wo_own, wo_sib, wi, act, hg, slope,
    held, part, rz_a, rz_b, ry_a, ry_b, acc, accb, in_send, in_recv,
    send_sem, recv_sem, local_sem,
):
    gx, gy = lax.axis_index("gx"), lax.axis_index("gy")
    x, zh = gx % 4, gx // 4
    core, z, y = gy % 2, (gy // 2) % 2, gy // 4

    def on_gy(dy, dz, dc=0):
        return ((y + dy) % 4) * 4 + ((z + dz) % 2) * 2 + (core + dc) % 2

    def on_gx(dx, dzh):
        return ((zh + dzh) % 2) * 4 + (x + dx) % 4

    YP, YM, Z, C = (gx, on_gy(1, 0)), (gx, on_gy(3, 0)), (gx, on_gy(0, 1)), (gx, on_gy(0, 0, 1))
    XP, XM, ZH = (on_gx(1, 0), gy), (on_gx(3, 0), gy), (on_gx(0, 1), gy)

    count = [0, 0]
    sent = []

    def send(src, dst, device):
        k = count[0]
        count[0] += 1
        copy = pltpu.make_async_remote_copy(
            src_ref=src, dst_ref=dst, send_sem=send_sem.at[k], recv_sem=recv_sem.at[k],
            device_id=device, device_id_type=MESH,
        )
        copy.start()
        sent.append(copy)
        return copy

    def local(src, dst):
        k = count[1]
        count[1] += 1
        copy = pltpu.make_async_copy(src, dst, local_sem.at[k])
        copy.start()
        return copy

    own_pre = local(pre_ref.at[:, pl.ds(pl.multiple_of(gy * UNITS, UNITS), UNITS)], preg.at[gy])
    load_wo = local(w_out_ref.at[:, core], wo_own)
    load_wi = local(w_in_ref, wi)
    barrier = pltpu.get_barrier_semaphore()
    for d in range(1, PIECES):
        pl.semaphore_signal(barrier, inc=1, device_id=(gx, (gy + d) % PIECES), device_id_type=MESH)
    for d in range(1, SHARDS):
        pl.semaphore_signal(barrier, inc=1, device_id=((gx + d) % SHARDS, gy), device_id_type=MESH)

    pl.semaphore_wait(barrier, PIECES - 1 + SHARDS - 1)

    lo, hi = pl.ds(0, ROWS // 2), pl.ds(ROWS // 2, ROWS // 2)

    def ring_start(src, buf):
        return send(src, buf.at[gx], ZH), send(src, buf.at[gx], XP), send(src, buf.at[gx], XM)

    def ring_relay(buf, first):
        def pass_on(dzh, to_right, to_left):
            to_right.wait_recv()
            came = on_gx(3, dzh)
            a = send(buf.at[came, lo], buf.at[came, lo], XP)
            to_left.wait_recv()
            came = on_gx(1, dzh)
            b = send(buf.at[came, hi], buf.at[came, hi], XM)
            return [a, b]

        across, right, left = first
        across.wait_recv()
        other = on_gx(0, 1)
        right2 = send(buf.at[other], buf.at[other], XP)
        left2 = send(buf.at[other], buf.at[other], XM)
        return pass_on(0, right, left) + pass_on(1, right2, left2)

    dy_first = ring_start(dy_ref, dyg)
    pre_copies = []
    for d in range(1, PIECES):
        to = (gy + d) % PIECES
        columns = pl.ds(pl.multiple_of(to * UNITS, UNITS), UNITS)
        pre_copies.append(send(pre_ref.at[:, columns], preg.at[gy], (gx, to)))
    swap_wo = send(w_out_ref.at[:, 1 - core], wo_sib, C)
    start = jnp.int32(0)
    for s in range(SHARDS):
        number = counts[s]

        def fill(i, carry, s=s, start=start, number=number):
            slot = lax.broadcasted_iota(jnp.int32, (16, LIVE), 0) + i * 16
            column = lax.broadcasted_iota(jnp.int32, (16, LIVE), 1)
            hit = (column == slot + start) & (slot < number)
            pt[pl.ds(pl.multiple_of(s * ROWS + i * 16, 16), 16), :] = jnp.where(hit, 1.0, 0.0).astype(BF16)
            return carry

        lax.fori_loop(0, ROWS // 16, fill, 0)
        start = start + number
    dyg[gx] = dy_ref[...]
    xg[gx] = x_ref[...]
    dy_last = ring_relay(dyg, dy_first)

    def compact(buf, width):
        whole = buf[...].reshape(SHARDS * ROWS, width)
        return dot(whole, pt[...], 0, 0)

    def split(ha):
        qa, qb = ha // 2, (UNITS - ha) // 2
        return (
            pl.ds(0, ha), pl.ds(ha, 2 * qb), pl.ds(0, qa), pl.ds(qa, qa), pl.ds(ha, qb), pl.ds(ha + qb, qb)
        )

    rows_a, rows_b, a0, a1, b0, b1 = split(HA)

    def gather_a(buf, ha):
        rows_a = split(ha)[0]
        own = buf.at[gy, rows_a]
        return {"z": send(own, own, Z), "+": send(own, own, YP), "-": send(own, own, YM), "c": send(own, own, C)}

    def gather_b(buf, ha):
        rows_b = split(ha)[1]
        own = buf.at[gy, rows_b]
        return {"+": send(own, own, YP), "-": send(own, own, YM), "z": send(own, own, Z), "c": send(own, own, C)}

    def gather_rest(buf, ha, fa, fb, use):
        rows_a, rows_b, a0, a1, b0, b1 = split(ha)
        sib = {(0, 0): [fa["c"], fb["c"]]}

        def fwd(dy, dz, rows, device):
            piece = buf.at[on_gy(dy, dz), rows]
            return send(piece, piece, device)

        def to_sibling(dy, dz, rows):
            sib.setdefault((dy, dz), []).append(fwd(dy, dz, rows, C))

        def done(dy, dz):
            for copy in sib[dy, dz]:
                copy.wait_recv()
            use(((y + dy) % 4) * 2 + (z + dz) % 2)

        fa["z"].wait_recv()
        plus = fwd(0, 1, rows_a, YP)
        minus = fwd(0, 1, rows_a, YM)
        to_sibling(0, 1, rows_a)
        fa["+"].wait_recv()
        a20p = fwd(3, 0, a0, YP)
        to_sibling(3, 0, rows_a)
        fa["-"].wait_recv()
        a20m = fwd(1, 0, a1, YM)
        to_sibling(1, 0, rows_a)
        fb["+"].wait_recv()
        b20p = fwd(3, 0, b0, YP)
        zm = fwd(3, 0, rows_b, Z)
        to_sibling(3, 0, rows_b)
        fb["-"].wait_recv()
        b20m = fwd(1, 0, b1, YM)
        zp = fwd(1, 0, rows_b, Z)
        to_sibling(1, 0, rows_b)
        yield
        done(0, 0)
        yield
        plus.wait_recv()
        a21p = fwd(3, 1, a0, YP)
        to_sibling(3, 1, rows_a)
        minus.wait_recv()
        a21m = fwd(1, 1, a1, YM)
        to_sibling(1, 1, rows_a)
        a20p.wait_recv()
        a20m.wait_recv()
        to_sibling(2, 0, rows_a)
        b20p.wait_recv()
        b20m.wait_recv()
        z2 = fwd(2, 0, rows_b, Z)
        to_sibling(2, 0, rows_b)
        fb["z"].wait_recv()
        to_sibling(0, 1, rows_b)
        done(3, 0)
        done(1, 0)
        zm.wait_recv()
        to_sibling(3, 1, rows_b)
        done(0, 1)
        a21p.wait_recv()
        a21m.wait_recv()
        to_sibling(2, 1, rows_a)
        zp.wait_recv()
        to_sibling(1, 1, rows_b)
        done(2, 0)
        done(3, 1)
        z2.wait_recv()
        to_sibling(2, 1, rows_b)
        done(1, 1)
        done(2, 1)
        yield

    own_pre.wait()
    for copy in pre_copies:
        copy.wait_recv()
    slope[...] = dot(preg[...].reshape(SHARDS * ROWS, UNITS), pt[...], 0, 0)

    def gelu(i, carry):
        rows = pl.ds(pl.multiple_of(i * 16, 16), 16)
        value, tilt = gelu_parts(slope[rows, :])
        act[gy, rows, :] = value.astype(BF16)
        slope[rows, :] = tilt
        return carry

    lax.fori_loop(0, UNITS // 16, gelu, 0)

    act_a = gather_a(act, HACT)
    act_b = gather_b(act, HACT)

    for copy in dy_last:
        copy.wait_recv()
    dyt[...] = compact(dyg, FEAT).astype(BF16)
    swap_dy = send(dyt, dys, C)
    x_first = ring_start(x_ref, xg)
    load_wo.wait()
    swap_wo.wait_recv()

    ring = {}

    def ring_send(key, dy, dz, q0, q1, land):
        if dy == 2:
            ring[key, "relay+"] = send(part.at[dy, dz, q0], land.at[0], YP)
            ring[key, "relay-"] = send(part.at[dy, dz, q1], land.at[1], YM)
        if dy == 1:
            ring[key, "direct+"] = send(part.at[dy, dz, q1], land.at[2], YP)
        if dy == 3:
            ring[key, "direct-"] = send(part.at[dy, dz, q0], land.at[3], YM)

    def ring_pass(key, dz, q0, q1, land):
        ring[key, "relay+"].wait_recv()
        part[1, dz, q0, :] = (held[1, dz, q0, :] + land[0].astype(F32)).astype(BF16)
        ring[key, "last+"] = send(part.at[1, dz, q0], land.at[4], YP)
        ring[key, "relay-"].wait_recv()
        part[3, dz, q1, :] = (held[3, dz, q1, :] + land[1].astype(F32)).astype(BF16)
        ring[key, "last-"] = send(part.at[3, dz, q1], land.at[5], YM)

    def ring_total(key, dz, q0, q1, land):
        ring[key, "direct-"].wait_recv()
        ring[key, "last+"].wait_recv()
        total0 = held[0, dz, q0, :] + land[3].astype(F32) + land[4].astype(F32)
        ring[key, "direct+"].wait_recv()
        ring[key, "last-"].wait_recv()
        total1 = held[0, dz, q1, :] + land[2].astype(F32) + land[5].astype(F32)
        return total0, total1

    swap_dy.wait_recv()
    z_copies = {}
    for dy, dz in ((2, 1), (2, 0), (1, 1), (3, 1), (0, 1), (1, 0), (3, 0), (0, 0)):
        chip = ((y + dy) % 4) * 2 + (z + dz) % 2
        total = dot(wo_own[chip], dyt[...], 1, 0) + dot(wo_sib[chip], dys[...], 1, 0)
        held[dy, dz] = total
        part[dy, dz] = total.astype(BF16)
        ring_send(("a", dz), dy, dz, a0, a1, ry_a.at[dz])
        if dz == 1:
            z_copies[dy] = send(part.at[dy, dz, rows_b], rz_b.at[dy], Z)

    for dz in (1, 0):
        ring_pass(("a", dz), dz, a0, a1, ry_a.at[dz])
    x_last = ring_relay(xg, x_first)
    for dy in (2, 1, 3, 0):
        z_copies[dy].wait_recv()
        total = held[dy, 0, rows_b, :] + rz_b[dy].astype(F32)
        held[dy, 0, rows_b, :] = total
        part[dy, 0, rows_b, :] = total.astype(BF16)
        ring_send("b", dy, 0, b0, b1, ry_b)
        if dy == 3:
            ring_pass("b", 0, b0, b1, ry_b)
    total0, total1 = ring_total(("a", 1), 1, a0, a1, ry_a.at[1])
    part[0, 1, a0, :] = total0.astype(BF16)
    part[0, 1, a1, :] = total1.astype(BF16)
    z_last = send(part.at[0, 1, rows_a], rz_a, Z)

    def use_act(chip):
        block = act[pl.ds(chip * 2, 2)].reshape(2 * UNITS, LIVE)
        wo_out[chip] = dot(block, dyt[...], 1, 1).astype(BF16)

    act_steps = gather_rest(act, HACT, act_a, act_b, use_act)
    next(act_steps)

    total0, total1 = ring_total("b", 0, b0, b1, ry_b)
    hg[gy, b0, :] = (total0 * slope[b0, :]).astype(BF16)
    hg[gy, b1, :] = (total1 * slope[b1, :]).astype(BF16)
    hg_b = gather_b(hg, HA)
    total0, total1 = ring_total(("a", 0), 0, a0, a1, ry_a.at[0])
    z_last.wait_recv()
    hg[gy, a0, :] = ((total0 + rz_a[a0, :].astype(F32)) * slope[a0, :]).astype(BF16)
    hg[gy, a1, :] = ((total1 + rz_a[a1, :].astype(F32)) * slope[a1, :]).astype(BF16)
    hg_a = gather_a(hg, HA)

    next(act_steps)
    for copy in x_last:
        copy.wait_recv()
    xt[...] = compact(xg, FEAT).astype(BF16)
    load_wi.wait()
    acc[...] = jnp.zeros_like(acc)

    def use_hg(chip):
        columns = pl.ds(pl.multiple_of(chip * 2 * UNITS, 2 * UNITS), 2 * UNITS)
        block = hg[pl.ds(chip * 2, 2)].reshape(2 * UNITS, LIVE)
        acc[...] += dot(wi[:, columns], block, 1, 0)
        wi_out[chip] = dot(xt[...], block, 1, 1).astype(BF16)

    for _ in gather_rest(hg, HA, hg_a, hg_b, use_hg):
        pass

    accb[...] = acc[...].astype(BF16)
    in_copies = []
    for d in range(1, SHARDS):
        to = (gx + d) % SHARDS
        rows = pl.ds(pl.multiple_of(to * ROWS, ROWS), ROWS)
        in_send[d - 1] = dot(pt[rows, :], accb[...], 1, 1).astype(BF16)
        in_copies.append(send(in_send.at[d - 1], in_recv.at[d - 1], (to, gy)))

    for _ in act_steps:
        pass

    total = dot(pt[pl.ds(pl.multiple_of(gx * ROWS, ROWS), ROWS), :], accb[...], 1, 1)
    for k, copy in enumerate(in_copies):
        copy.wait_recv()
        total = total + in_recv[k].astype(F32)
    in_out[...] = total.astype(BF16)
    for copy in sent:
        copy.wait_send()


def store_kernel(in_ref, wi_ref, wo_ref, in_out, wi_out, wo_out, sem):
    copies = [pltpu.make_async_copy(in_ref, in_out, sem.at[16])]
    for chip in range(8):
        span = pl.ds(chip * 2 * UNITS, 2 * UNITS)
        copies.append(pltpu.make_async_copy(wi_ref.at[chip], wi_out.at[:, span], sem.at[chip]))
        copies.append(pltpu.make_async_copy(wo_ref.at[chip], wo_out.at[span], sem.at[8 + chip]))
    for copy in copies:
        copy.start()
    for copy in copies:
        copy.wait()


def body(inputs, out_grad, pre_act, w_in, w_out, counts):
    vmem = pl.BlockSpec(memory_space=pltpu.VMEM)
    anywhere = pl.BlockSpec(memory_space=pl.ANY)
    qa, qb = HA // 2, HB // 2
    flops = 2 * 4 * LIVE * FEAT * UNITS * PIECES
    results = pl.pallas_call(
        kernel,
        out_shape=(
            pltpu.VMEM((ROWS, FEAT), BF16),
            pltpu.VMEM((8, FEAT, 2 * UNITS), BF16),
            pltpu.VMEM((8, 2 * UNITS, FEAT), BF16),
        ),
        in_specs=[pl.BlockSpec(memory_space=pltpu.SMEM), vmem, vmem, anywhere, anywhere, anywhere],
        out_specs=(vmem, vmem, vmem),
        scratch_shapes=[
            pltpu.VMEM((SHARDS * ROWS, LIVE), BF16),
            pltpu.VMEM((SHARDS, ROWS, FEAT), BF16),
            pltpu.VMEM((SHARDS, ROWS, FEAT), BF16),
            pltpu.VMEM((PIECES, SHARDS * ROWS // PIECES, UNITS), BF16),
            pltpu.VMEM((FEAT, LIVE), BF16),
            pltpu.VMEM((FEAT, LIVE), BF16),
            pltpu.VMEM((FEAT, LIVE), BF16),
            pltpu.VMEM((8, UNITS, FEAT), BF16),
            pltpu.VMEM((8, UNITS, FEAT), BF16),
            pltpu.VMEM((FEAT, PIECES * UNITS), BF16),
            pltpu.VMEM((PIECES, UNITS, LIVE), BF16),
            pltpu.VMEM((PIECES, UNITS, LIVE), BF16),
            pltpu.VMEM((UNITS, LIVE), F32),
            pltpu.VMEM((4, 2, UNITS, LIVE), F32),
            pltpu.VMEM((4, 2, UNITS, LIVE), BF16),
            pltpu.VMEM((HA, LIVE), BF16),
            pltpu.VMEM((4, HB, LIVE), BF16),
            pltpu.VMEM((2, 6, qa, LIVE), BF16),
            pltpu.VMEM((6, qb, LIVE), BF16),
            pltpu.VMEM((FEAT, LIVE), F32),
            pltpu.VMEM((FEAT, LIVE), BF16),
            pltpu.VMEM((SHARDS - 1, ROWS, FEAT), BF16),
            pltpu.VMEM((SHARDS - 1, ROWS, FEAT), BF16),
            pltpu.SemaphoreType.DMA((144,)),
            pltpu.SemaphoreType.DMA((144,)),
            pltpu.SemaphoreType.DMA((3,)),
        ],
        compiler_params=pltpu.CompilerParams(
            collective_id=0, has_side_effects=True, vmem_limit_bytes=48 * 1024 * 1024
        ),
        cost_estimate=pl.CostEstimate(flops=flops, bytes_accessed=16 << 20, transcendentals=UNITS * LIVE),
        name="ffn_backward",
    )(counts, inputs, out_grad, pre_act, w_in, w_out.reshape(8, 2, UNITS, FEAT))
    return pl.pallas_call(
        store_kernel,
        out_shape=(
            jax.ShapeDtypeStruct((ROWS, FEAT), BF16),
            jax.ShapeDtypeStruct((FEAT, PIECES * UNITS), BF16),
            jax.ShapeDtypeStruct((PIECES * UNITS, FEAT), BF16),
        ),
        in_specs=[vmem, vmem, vmem],
        out_specs=(anywhere, anywhere, anywhere),
        scratch_shapes=[pltpu.SemaphoreType.DMA((17,))],
        compiler_params=pltpu.CompilerParams(vmem_limit_bytes=16 * 1024 * 1024),
        name="store_results",
    )(*results)


def solution(mesh):
    return jax.shard_map(
        body,
        mesh=mesh,
        in_specs=(P("gx", "gy"), P("gx", "gy"), P("gy", "gx"), P("gy", "gx"), P("gx", "gy"), P()),
        out_specs=(P("gx", "gy"), P("gy", "gx"), P("gx", "gy")),
        check_vma=False,
    )
```

```python
import math

import jax
import jax.numpy as jnp
from jax import lax
from jax.experimental import pallas as pl
from jax.experimental.pallas import tpu as pltpu
from jax.sharding import PartitionSpec as P

LIVE = 640
SHARDS = 8
ROWS = 128
FEAT = 512
PIECES = 16
UNITS = 256
HA = 160
HACT = 192
HB = UNITS - HA
MESH = pl.DeviceIdType.MESH
BF16, F32 = jnp.bfloat16, jnp.float32

gelu_scale = math.sqrt(2.0 / math.pi)
cubic_coef = 0.044715


def gelu_parts(pre):
    tangent = jnp.tanh(gelu_scale * (pre + cubic_coef * pre * pre * pre))
    value = 0.5 * pre * (1.0 + tangent)
    slope = 0.5 * (1.0 + tangent) + 0.5 * pre * (1.0 - tangent * tangent) * gelu_scale * (
        1.0 + 3.0 * cubic_coef * pre * pre
    )
    return value, slope


def dot(left, right, left_dim, right_dim):
    return lax.dot_general(
        left, right, (((left_dim,), (right_dim,)), ((), ())), preferred_element_type=F32
    )


def kernel(
    counts, x_ref, dy_ref, pre_ref, w_in_ref, w_out_ref,
    in_out, wi_out, wo_out,
    pt, dyg, xg, preg, dyt, dys, xt, wo_own, wo_sib, wi, act, hg, slope,
    held, part, rz_a, rz_b, ry_a, ry_b, acc, accb, left_part, right_part, left_x, left_send, left_z, right_z, right_send, right_x,
    send_sem, recv_sem, local_sem,
):
    gx, gy = lax.axis_index("gx"), lax.axis_index("gy")
    x, zh = gx % 4, gx // 4
    core, z, y = gy % 2, (gy // 2) % 2, gy // 4

    def on_gy(dy, dz, dc=0):
        return ((y + dy) % 4) * 4 + ((z + dz) % 2) * 2 + (core + dc) % 2

    def on_gx(dx, dzh):
        return ((zh + dzh) % 2) * 4 + (x + dx) % 4

    YP, YM, Z, C = (gx, on_gy(1, 0)), (gx, on_gy(3, 0)), (gx, on_gy(0, 1)), (gx, on_gy(0, 0, 1))
    XP, XM, ZH = (on_gx(1, 0), gy), (on_gx(3, 0), gy), (on_gx(0, 1), gy)

    count = [0, 0]
    sent = []

    def send(src, dst, device):
        k = count[0]
        count[0] += 1
        copy = pltpu.make_async_remote_copy(
            src_ref=src, dst_ref=dst, send_sem=send_sem.at[k], recv_sem=recv_sem.at[k],
            device_id=device, device_id_type=MESH,
        )
        copy.start()
        sent.append(copy)
        return copy

    def local(src, dst):
        k = count[1]
        count[1] += 1
        copy = pltpu.make_async_copy(src, dst, local_sem.at[k])
        copy.start()
        return copy

    own_pre = local(pre_ref.at[:, pl.ds(pl.multiple_of(gy * UNITS, UNITS), UNITS)], preg.at[gy])
    own_dy, own_x = local(dy_ref, dyg.at[gx]), local(x_ref, xg.at[gx])
    load_wo = local(w_out_ref.at[:, core], wo_own)
    load_wi = local(w_in_ref, wi)
    barrier = pltpu.get_barrier_semaphore()
    for d in range(1, PIECES):
        pl.semaphore_signal(barrier, inc=1, device_id=(gx, (gy + d) % PIECES), device_id_type=MESH)
    for d in range(1, SHARDS):
        pl.semaphore_signal(barrier, inc=1, device_id=((gx + d) % SHARDS, gy), device_id_type=MESH)

    pl.semaphore_wait(barrier, PIECES - 1 + SHARDS - 1)

    lo, hi = pl.ds(0, ROWS // 2), pl.ds(ROWS // 2, ROWS // 2)

    def ring_start(src, buf):
        return send(src, buf.at[gx], ZH), send(src, buf.at[gx], XP), send(src, buf.at[gx], XM)

    def ring_relay(buf, first):
        def pass_on(dzh, to_right, to_left):
            to_right.wait_recv()
            came = on_gx(3, dzh)
            a = send(buf.at[came, lo], buf.at[came, lo], XP)
            to_left.wait_recv()
            came = on_gx(1, dzh)
            b = send(buf.at[came, hi], buf.at[came, hi], XM)
            return [a, b]

        across, right, left = first
        across.wait_recv()
        other = on_gx(0, 1)
        right2 = send(buf.at[other], buf.at[other], XP)
        left2 = send(buf.at[other], buf.at[other], XM)
        return pass_on(0, right, left) + pass_on(1, right2, left2)

    dy_first = ring_start(dy_ref, dyg)
    pre_copies = []
    for d in range(1, PIECES):
        to = (gy + d) % PIECES
        columns = pl.ds(pl.multiple_of(to * UNITS, UNITS), UNITS)
        pre_copies.append(send(pre_ref.at[:, columns], preg.at[gy], (gx, to)))
    swap_wo = send(w_out_ref.at[:, 1 - core], wo_sib, C)
    start = jnp.int32(0)
    for s in range(SHARDS):
        number = counts[s]

        def fill(i, carry, s=s, start=start, number=number):
            slot = lax.broadcasted_iota(jnp.int32, (16, LIVE), 0) + i * 16
            column = lax.broadcasted_iota(jnp.int32, (16, LIVE), 1)
            hit = (column == slot + start) & (slot < number)
            pt[pl.ds(pl.multiple_of(s * ROWS + i * 16, 16), 16), :] = jnp.where(hit, 1.0, 0.0).astype(BF16)
            return carry

        lax.fori_loop(0, ROWS // 16, fill, 0)
        start = start + number
    dy_last = ring_relay(dyg, dy_first)

    def compact(buf, width):
        whole = buf[...].reshape(SHARDS * ROWS, width)
        return dot(whole, pt[...], 0, 0)

    def split(ha):
        qa, qb = ha // 2, (UNITS - ha) // 2
        return (
            pl.ds(0, ha), pl.ds(ha, 2 * qb), pl.ds(0, qa), pl.ds(qa, qa), pl.ds(ha, qb), pl.ds(ha + qb, qb)
        )

    rows_a, rows_b, a0, a1, b0, b1 = split(HA)

    def gather_a(buf, ha):
        rows_a = split(ha)[0]
        own = buf.at[gy, rows_a]
        return {"z": send(own, own, Z), "+": send(own, own, YP), "-": send(own, own, YM), "c": send(own, own, C)}

    def gather_b(buf, ha):
        rows_b = split(ha)[1]
        own = buf.at[gy, rows_b]
        return {"+": send(own, own, YP), "-": send(own, own, YM), "z": send(own, own, Z), "c": send(own, own, C)}

    def gather_rest(buf, ha, fa, fb, use):
        rows_a, rows_b, a0, a1, b0, b1 = split(ha)
        sib = {(0, 0): [fa["c"], fb["c"]]}

        def fwd(dy, dz, rows, device):
            piece = buf.at[on_gy(dy, dz), rows]
            return send(piece, piece, device)

        def to_sibling(dy, dz, rows):
            sib.setdefault((dy, dz), []).append(fwd(dy, dz, rows, C))

        def done(dy, dz):
            for copy in sib[dy, dz]:
                copy.wait_recv()
            use(((y + dy) % 4) * 2 + (z + dz) % 2)

        fa["z"].wait_recv()
        plus = fwd(0, 1, rows_a, YP)
        minus = fwd(0, 1, rows_a, YM)
        to_sibling(0, 1, rows_a)
        fa["+"].wait_recv()
        a20p = fwd(3, 0, a0, YP)
        to_sibling(3, 0, rows_a)
        fa["-"].wait_recv()
        a20m = fwd(1, 0, a1, YM)
        to_sibling(1, 0, rows_a)
        fb["+"].wait_recv()
        b20p = fwd(3, 0, b0, YP)
        zm = fwd(3, 0, rows_b, Z)
        to_sibling(3, 0, rows_b)
        fb["-"].wait_recv()
        b20m = fwd(1, 0, b1, YM)
        zp = fwd(1, 0, rows_b, Z)
        to_sibling(1, 0, rows_b)
        yield
        done(0, 0)
        yield
        plus.wait_recv()
        a21p = fwd(3, 1, a0, YP)
        to_sibling(3, 1, rows_a)
        minus.wait_recv()
        a21m = fwd(1, 1, a1, YM)
        to_sibling(1, 1, rows_a)
        a20p.wait_recv()
        a20m.wait_recv()
        to_sibling(2, 0, rows_a)
        b20p.wait_recv()
        b20m.wait_recv()
        z2 = fwd(2, 0, rows_b, Z)
        to_sibling(2, 0, rows_b)
        fb["z"].wait_recv()
        to_sibling(0, 1, rows_b)
        done(3, 0)
        done(1, 0)
        yield
        zm.wait_recv()
        to_sibling(3, 1, rows_b)
        done(0, 1)
        a21p.wait_recv()
        a21m.wait_recv()
        to_sibling(2, 1, rows_a)
        zp.wait_recv()
        to_sibling(1, 1, rows_b)
        done(2, 0)
        done(3, 1)
        z2.wait_recv()
        to_sibling(2, 1, rows_b)
        done(1, 1)
        done(2, 1)
        yield

    own_pre.wait()
    for copy in pre_copies:
        copy.wait_recv()
    slope[...] = dot(preg[...].reshape(SHARDS * ROWS, UNITS), pt[...], 0, 0)

    def gelu(i, carry):
        rows = pl.ds(pl.multiple_of(i * 16, 16), 16)
        value, tilt = gelu_parts(slope[rows, :])
        act[gy, rows, :] = value.astype(BF16)
        slope[rows, :] = tilt
        return carry

    lax.fori_loop(0, UNITS // 16, gelu, 0)

    act_a = gather_a(act, HACT)
    act_b = gather_b(act, HACT)

    for copy in dy_last:
        copy.wait_recv()
    own_dy.wait()
    dyt[...] = compact(dyg, FEAT).astype(BF16)
    swap_dy = send(dyt, dys, C)
    x_first = ring_start(x_ref, xg)
    load_wo.wait()
    swap_wo.wait_recv()

    ring = {}

    def ring_send(key, dy, dz, q0, q1, land):
        if dy == 2:
            ring[key, "relay+"] = send(part.at[dy, dz, q0], land.at[0], YP)
            ring[key, "relay-"] = send(part.at[dy, dz, q1], land.at[1], YM)
        if dy == 1:
            ring[key, "direct+"] = send(part.at[dy, dz, q1], land.at[2], YP)
        if dy == 3:
            ring[key, "direct-"] = send(part.at[dy, dz, q0], land.at[3], YM)

    def ring_pass(key, dz, q0, q1, land):
        ring[key, "relay+"].wait_recv()
        part[1, dz, q0, :] = (held[1, dz, q0, :] + land[0].astype(F32)).astype(BF16)
        ring[key, "last+"] = send(part.at[1, dz, q0], land.at[4], YP)
        ring[key, "relay-"].wait_recv()
        part[3, dz, q1, :] = (held[3, dz, q1, :] + land[1].astype(F32)).astype(BF16)
        ring[key, "last-"] = send(part.at[3, dz, q1], land.at[5], YM)

    def ring_total(key, dz, q0, q1, land):
        ring[key, "direct-"].wait_recv()
        ring[key, "last+"].wait_recv()
        total0 = held[0, dz, q0, :] + land[3].astype(F32) + land[4].astype(F32)
        ring[key, "direct+"].wait_recv()
        ring[key, "last-"].wait_recv()
        total1 = held[0, dz, q1, :] + land[2].astype(F32) + land[5].astype(F32)
        return total0, total1

    swap_dy.wait_recv()
    z_copies = {}
    for dy, dz in ((2, 1), (2, 0), (1, 1), (3, 1), (0, 1), (1, 0), (3, 0), (0, 0)):
        chip = ((y + dy) % 4) * 2 + (z + dz) % 2
        total = dot(wo_own[chip], dyt[...], 1, 0) + dot(wo_sib[chip], dys[...], 1, 0)
        held[dy, dz] = total
        part[dy, dz] = total.astype(BF16)
        ring_send(("a", dz), dy, dz, a0, a1, ry_a.at[dz])
        if dz == 1:
            z_copies[dy] = send(part.at[dy, dz, rows_b], rz_b.at[dy], Z)

    for dz in (1, 0):
        ring_pass(("a", dz), dz, a0, a1, ry_a.at[dz])
    x_last = ring_relay(xg, x_first)
    for dy in (2, 1, 3, 0):
        z_copies[dy].wait_recv()
        total = held[dy, 0, rows_b, :] + rz_b[dy].astype(F32)
        held[dy, 0, rows_b, :] = total
        part[dy, 0, rows_b, :] = total.astype(BF16)
        ring_send("b", dy, 0, b0, b1, ry_b)
        if dy == 3:
            ring_pass("b", 0, b0, b1, ry_b)
    total0, total1 = ring_total(("a", 1), 1, a0, a1, ry_a.at[1])
    part[0, 1, a0, :] = total0.astype(BF16)
    part[0, 1, a1, :] = total1.astype(BF16)
    z_last = send(part.at[0, 1, rows_a], rz_a, Z)

    def use_act(chip):
        block = act[pl.ds(chip * 2, 2)].reshape(2 * UNITS, LIVE)
        wo_out[chip] = dot(block, dyt[...], 1, 1).astype(BF16)

    act_steps = gather_rest(act, HACT, act_a, act_b, use_act)
    next(act_steps)

    total0, total1 = ring_total("b", 0, b0, b1, ry_b)
    hg[gy, b0, :] = (total0 * slope[b0, :]).astype(BF16)
    hg[gy, b1, :] = (total1 * slope[b1, :]).astype(BF16)
    hg_b = gather_b(hg, HA)
    total0, total1 = ring_total(("a", 0), 0, a0, a1, ry_a.at[0])
    z_last.wait_recv()
    hg[gy, a0, :] = ((total0 + rz_a[a0, :].astype(F32)) * slope[a0, :]).astype(BF16)
    hg[gy, a1, :] = ((total1 + rz_a[a1, :].astype(F32)) * slope[a1, :]).astype(BF16)
    hg_a = gather_a(hg, HA)

    next(act_steps)
    for copy in x_last:
        copy.wait_recv()
    own_x.wait()
    xt[...] = compact(xg, FEAT).astype(BF16)
    load_wi.wait()
    acc[...] = jnp.zeros_like(acc)

    late = []

    def block_of(buf, chip):
        return buf[pl.ds(chip * 2, 2)].reshape(2 * UNITS, LIVE)

    def use_hg(chip):
        columns = pl.ds(pl.multiple_of(chip * 2 * UNITS, 2 * UNITS), 2 * UNITS)
        block = block_of(hg, chip)
        acc[...] += dot(wi[:, columns], block, 1, 0)
        late.append(chip)
        if len(late) <= 4:
            wi_out[chip] = dot(xt[...], block, 1, 1).astype(BF16)

    hg_steps = gather_rest(hg, HA, hg_a, hg_b, use_hg)
    for _ in range(3):
        next(hg_steps)
    next(act_steps)
    next(hg_steps)

    half = FEAT // 2
    accb[...] = acc[...].astype(BF16)
    right_part[...] = dot(pt[...], accb[half:, :], 1, 1).astype(BF16).reshape(SHARDS, ROWS, half)
    far = pl.ds((1 - zh) * 4, 4)
    right_copy = send(right_part.at[far], right_z, ZH)
    left_part[...] = dot(pt[...], accb[:half, :], 1, 1).astype(BF16).reshape(SHARDS, ROWS, half)
    left_copies = [
        send(left_part.at[on_gx(d, dzh)], left_x.at[dzh, d - 1], (on_gx(d, 0), gy))
        for dzh in (1, 0) for d in (1, 2, 3)
    ]
    for chip in late[4:]:
        wi_out[chip] = dot(xt[...], block_of(hg, chip), 1, 1).astype(BF16)
    right_copy.wait_recv()
    right_last = []
    for d in (2, 1, 3):
        right_send[d - 1] = (
            right_part[on_gx(d, 0)].astype(F32) + right_z[(x + d) % 4].astype(F32)
        ).astype(BF16)
        right_last.append(send(right_send.at[d - 1], right_x.at[d - 1], (on_gx(d, 0), gy)))
    for copy in left_copies[:3]:
        copy.wait_recv()
    total = left_part[on_gx(0, 1)].astype(F32)
    for d in range(3):
        total = total + left_x[1, d].astype(F32)
    left_send[...] = total.astype(BF16)
    left_last = send(left_send, left_z, ZH)

    for _ in act_steps:
        pass

    for copy in left_copies[3:] + right_last + [left_last]:
        copy.wait_recv()
    total = left_part[gx].astype(F32) + left_z[...].astype(F32)
    for d in range(3):
        total = total + left_x[0, d].astype(F32)
    in_out[:, :half] = total.astype(BF16)
    total = right_part[gx].astype(F32) + right_z[x].astype(F32)
    for d in range(3):
        total = total + right_x[d].astype(F32)
    in_out[:, half:] = total.astype(BF16)
    for copy in sent:
        copy.wait_send()


def store_kernel(in_ref, wi_ref, wo_ref, in_out, wi_out, wo_out, sem):
    copies = [pltpu.make_async_copy(in_ref, in_out, sem.at[16])]
    for chip in range(8):
        span = pl.ds(chip * 2 * UNITS, 2 * UNITS)
        copies.append(pltpu.make_async_copy(wi_ref.at[chip], wi_out.at[:, span], sem.at[chip]))
        copies.append(pltpu.make_async_copy(wo_ref.at[chip], wo_out.at[span], sem.at[8 + chip]))
    for copy in copies:
        copy.start()
    for copy in copies:
        copy.wait()


def body(inputs, out_grad, pre_act, w_in, w_out, counts):
    vmem = pl.BlockSpec(memory_space=pltpu.VMEM)
    anywhere = pl.BlockSpec(memory_space=pl.ANY)
    qa, qb = HA // 2, HB // 2
    flops = 2 * 4 * LIVE * FEAT * UNITS * PIECES
    results = pl.pallas_call(
        kernel,
        out_shape=(
            pltpu.VMEM((ROWS, FEAT), BF16),
            pltpu.VMEM((8, FEAT, 2 * UNITS), BF16),
            pltpu.VMEM((8, 2 * UNITS, FEAT), BF16),
        ),
        in_specs=[pl.BlockSpec(memory_space=pltpu.SMEM)] + [anywhere] * 5,
        out_specs=(vmem, vmem, vmem),
        scratch_shapes=[
            pltpu.VMEM((SHARDS * ROWS, LIVE), BF16),
            pltpu.VMEM((SHARDS, ROWS, FEAT), BF16),
            pltpu.VMEM((SHARDS, ROWS, FEAT), BF16),
            pltpu.VMEM((PIECES, SHARDS * ROWS // PIECES, UNITS), BF16),
            pltpu.VMEM((FEAT, LIVE), BF16),
            pltpu.VMEM((FEAT, LIVE), BF16),
            pltpu.VMEM((FEAT, LIVE), BF16),
            pltpu.VMEM((8, UNITS, FEAT), BF16),
            pltpu.VMEM((8, UNITS, FEAT), BF16),
            pltpu.VMEM((FEAT, PIECES * UNITS), BF16),
            pltpu.VMEM((PIECES, UNITS, LIVE), BF16),
            pltpu.VMEM((PIECES, UNITS, LIVE), BF16),
            pltpu.VMEM((UNITS, LIVE), F32),
            pltpu.VMEM((4, 2, UNITS, LIVE), F32),
            pltpu.VMEM((4, 2, UNITS, LIVE), BF16),
            pltpu.VMEM((HA, LIVE), BF16),
            pltpu.VMEM((4, HB, LIVE), BF16),
            pltpu.VMEM((2, 6, qa, LIVE), BF16),
            pltpu.VMEM((6, qb, LIVE), BF16),
            pltpu.VMEM((FEAT, LIVE), F32),
            pltpu.VMEM((FEAT, LIVE), BF16),
            pltpu.VMEM((SHARDS, ROWS, FEAT // 2), BF16),
            pltpu.VMEM((SHARDS, ROWS, FEAT // 2), BF16),
            pltpu.VMEM((2, 3, ROWS, FEAT // 2), BF16),
            pltpu.VMEM((ROWS, FEAT // 2), BF16),
            pltpu.VMEM((ROWS, FEAT // 2), BF16),
            pltpu.VMEM((4, ROWS, FEAT // 2), BF16),
            pltpu.VMEM((3, ROWS, FEAT // 2), BF16),
            pltpu.VMEM((3, ROWS, FEAT // 2), BF16),
            pltpu.SemaphoreType.DMA((144,)),
            pltpu.SemaphoreType.DMA((144,)),
            pltpu.SemaphoreType.DMA((5,)),
        ],
        compiler_params=pltpu.CompilerParams(
            collective_id=0, has_side_effects=True, vmem_limit_bytes=48 * 1024 * 1024
        ),
        cost_estimate=pl.CostEstimate(flops=flops, bytes_accessed=16 << 20, transcendentals=UNITS * LIVE),
        name="ffn_backward",
    )(counts, inputs, out_grad, pre_act, w_in, w_out.reshape(8, 2, UNITS, FEAT))
    return pl.pallas_call(
        store_kernel,
        out_shape=(
            jax.ShapeDtypeStruct((ROWS, FEAT), BF16),
            jax.ShapeDtypeStruct((FEAT, PIECES * UNITS), BF16),
            jax.ShapeDtypeStruct((PIECES * UNITS, FEAT), BF16),
        ),
        in_specs=[vmem, vmem, vmem],
        out_specs=(anywhere, anywhere, anywhere),
        scratch_shapes=[pltpu.SemaphoreType.DMA((17,))],
        compiler_params=pltpu.CompilerParams(vmem_limit_bytes=16 * 1024 * 1024),
        name="store_results",
    )(*results)


def solution(mesh):
    return jax.shard_map(
        body,
        mesh=mesh,
        in_specs=(P("gx", "gy"), P("gx", "gy"), P("gy", "gx"), P("gy", "gx"), P("gx", "gy"), P()),
        out_specs=(P("gx", "gy"), P("gy", "gx"), P("gx", "gy")),
        check_vma=False,
    )
```

```python
import math

import jax
import jax.numpy as jnp
from jax import lax
from jax.experimental import pallas as pl
from jax.experimental.pallas import tpu as pltpu
from jax.sharding import PartitionSpec as P

LIVE = 640
SHARDS = 8
ROWS = 128
FEAT = 512
PIECES = 16
UNITS = 256
HA = 160
HACT = 192
HB = UNITS - HA
MESH = pl.DeviceIdType.MESH
BF16, F32 = jnp.bfloat16, jnp.float32

gelu_scale = math.sqrt(2.0 / math.pi)
cubic_coef = 0.044715


def gelu_parts(pre):
    tangent = jnp.tanh(gelu_scale * (pre + cubic_coef * pre * pre * pre))
    value = 0.5 * pre * (1.0 + tangent)
    slope = 0.5 * (1.0 + tangent) + 0.5 * pre * (1.0 - tangent * tangent) * gelu_scale * (
        1.0 + 3.0 * cubic_coef * pre * pre
    )
    return value, slope


def dot(left, right, left_dim, right_dim):
    return lax.dot_general(
        left, right, (((left_dim,), (right_dim,)), ((), ())), preferred_element_type=F32
    )


def kernel(
    counts, x_ref, dy_ref, pre_ref, w_in_ref, w_out_ref,
    in_out, wi_out, wo_out,
    pt, dyg, xg, preg, dyt, dys, xt, wo_own, wo_sib, wi, act, hg, slope,
    held, part, rz_a, rz_b, ry_a, ry_b, acc, accb, left_part, right_part, left_x, left_send, left_z, right_z, right_send, right_x,
    send_sem, recv_sem, local_sem,
):
    gx, gy = lax.axis_index("gx"), lax.axis_index("gy")
    x, zh = gx % 4, gx // 4
    core, z, y = gy % 2, (gy // 2) % 2, gy // 4

    def on_gy(dy, dz, dc=0):
        return ((y + dy) % 4) * 4 + ((z + dz) % 2) * 2 + (core + dc) % 2

    def on_gx(dx, dzh):
        return ((zh + dzh) % 2) * 4 + (x + dx) % 4

    YP, YM, Z, C = (gx, on_gy(1, 0)), (gx, on_gy(3, 0)), (gx, on_gy(0, 1)), (gx, on_gy(0, 0, 1))
    XP, XM, ZH = (on_gx(1, 0), gy), (on_gx(3, 0), gy), (on_gx(0, 1), gy)

    count = [0, 0]
    sent = []

    def send(src, dst, device):
        k = count[0]
        count[0] += 1
        copy = pltpu.make_async_remote_copy(
            src_ref=src, dst_ref=dst, send_sem=send_sem.at[k], recv_sem=recv_sem.at[k],
            device_id=device, device_id_type=MESH,
        )
        copy.start()
        sent.append(copy)
        return copy

    def local(src, dst):
        k = count[1]
        count[1] += 1
        copy = pltpu.make_async_copy(src, dst, local_sem.at[k])
        copy.start()
        return copy

    own_pre = local(pre_ref.at[:, pl.ds(pl.multiple_of(gy * UNITS, UNITS), UNITS)], preg.at[gy])
    own_dy, own_x = local(dy_ref, dyg.at[gx]), local(x_ref, xg.at[gx])
    load_wo = local(w_out_ref.at[:, core], wo_own)
    load_wi = local(w_in_ref, wi)
    barrier = pltpu.get_barrier_semaphore()
    for d in range(1, PIECES):
        pl.semaphore_signal(barrier, inc=1, device_id=(gx, (gy + d) % PIECES), device_id_type=MESH)
    for d in range(1, SHARDS):
        pl.semaphore_signal(barrier, inc=1, device_id=((gx + d) % SHARDS, gy), device_id_type=MESH)

    pl.semaphore_wait(barrier, PIECES - 1 + SHARDS - 1)

    def ring_start(src, buf, chunks):
        size = ROWS // chunks
        return [
            [send(src.at[pl.ds(k * size, size)], buf.at[gx, pl.ds(k * size, size)], to) for to in (ZH, XP, XM)]
            for k in range(chunks)
        ]

    def ring_relay(buf, first):
        size = ROWS // len(first)
        last, second = [], []

        def pass_on(k, dzh, to_right, to_left):
            to_right.wait_recv()
            piece = buf.at[on_gx(3, dzh), pl.ds(k * size, size // 2)]
            last.append(send(piece, piece, XP))
            to_left.wait_recv()
            piece = buf.at[on_gx(1, dzh), pl.ds(k * size + size // 2, size // 2)]
            last.append(send(piece, piece, XM))

        for k, (across, right, left) in enumerate(first):
            across.wait_recv()
            piece = buf.at[on_gx(0, 1), pl.ds(k * size, size)]
            second.append((send(piece, piece, XP), send(piece, piece, XM)))
            pass_on(k, 0, right, left)
        for k, (right, left) in enumerate(second):
            pass_on(k, 1, right, left)
        return last

    dy_first = ring_start(dy_ref, dyg, 2)
    pre_copies = []
    for d in range(1, PIECES):
        to = (gy + d) % PIECES
        columns = pl.ds(pl.multiple_of(to * UNITS, UNITS), UNITS)
        pre_copies.append(send(pre_ref.at[:, columns], preg.at[gy], (gx, to)))
    swap_wo = send(w_out_ref.at[:, 1 - core], wo_sib, C)
    start = jnp.int32(0)
    for s in range(SHARDS):
        number = counts[s]

        def fill(i, carry, s=s, start=start, number=number):
            slot = lax.broadcasted_iota(jnp.int32, (16, LIVE), 0) + i * 16
            column = lax.broadcasted_iota(jnp.int32, (16, LIVE), 1)
            hit = (column == slot + start) & (slot < number)
            pt[pl.ds(pl.multiple_of(s * ROWS + i * 16, 16), 16), :] = jnp.where(hit, 1.0, 0.0).astype(BF16)
            return carry

        lax.fori_loop(0, ROWS // 16, fill, 0)
        start = start + number
    dy_last = ring_relay(dyg, dy_first)

    def compact(buf, width):
        whole = buf[...].reshape(SHARDS * ROWS, width)
        return dot(whole, pt[...], 0, 0)

    def split(ha):
        qa, qb = ha // 2, (UNITS - ha) // 2
        return (
            pl.ds(0, ha), pl.ds(ha, 2 * qb), pl.ds(0, qa), pl.ds(qa, qa), pl.ds(ha, qb), pl.ds(ha + qb, qb)
        )

    rows_a, rows_b, a0, a1, b0, b1 = split(HA)

    def gather_a(buf, ha):
        rows_a = split(ha)[0]
        own = buf.at[gy, rows_a]
        return {"z": send(own, own, Z), "+": send(own, own, YP), "-": send(own, own, YM), "c": send(own, own, C)}

    def gather_b(buf, ha):
        rows_b = split(ha)[1]
        own = buf.at[gy, rows_b]
        return {"+": send(own, own, YP), "-": send(own, own, YM), "z": send(own, own, Z), "c": send(own, own, C)}

    def gather_rest(buf, ha, fa, fb, use):
        rows_a, rows_b, a0, a1, b0, b1 = split(ha)
        sib = {(0, 0): [fa["c"], fb["c"]]}

        def fwd(dy, dz, rows, device):
            piece = buf.at[on_gy(dy, dz), rows]
            return send(piece, piece, device)

        def to_sibling(dy, dz, rows):
            sib.setdefault((dy, dz), []).append(fwd(dy, dz, rows, C))

        def done(dy, dz):
            for copy in sib[dy, dz]:
                copy.wait_recv()
            use(((y + dy) % 4) * 2 + (z + dz) % 2)

        fa["z"].wait_recv()
        plus = fwd(0, 1, rows_a, YP)
        minus = fwd(0, 1, rows_a, YM)
        to_sibling(0, 1, rows_a)
        fa["+"].wait_recv()
        a20p = fwd(3, 0, a0, YP)
        to_sibling(3, 0, rows_a)
        fa["-"].wait_recv()
        a20m = fwd(1, 0, a1, YM)
        to_sibling(1, 0, rows_a)
        fb["+"].wait_recv()
        b20p = fwd(3, 0, b0, YP)
        zm = fwd(3, 0, rows_b, Z)
        to_sibling(3, 0, rows_b)
        fb["-"].wait_recv()
        b20m = fwd(1, 0, b1, YM)
        zp = fwd(1, 0, rows_b, Z)
        to_sibling(1, 0, rows_b)
        yield
        done(0, 0)
        yield
        plus.wait_recv()
        a21p = fwd(3, 1, a0, YP)
        to_sibling(3, 1, rows_a)
        minus.wait_recv()
        a21m = fwd(1, 1, a1, YM)
        to_sibling(1, 1, rows_a)
        a20p.wait_recv()
        a20m.wait_recv()
        to_sibling(2, 0, rows_a)
        b20p.wait_recv()
        b20m.wait_recv()
        z2 = fwd(2, 0, rows_b, Z)
        to_sibling(2, 0, rows_b)
        fb["z"].wait_recv()
        to_sibling(0, 1, rows_b)
        done(3, 0)
        done(1, 0)
        yield
        zm.wait_recv()
        to_sibling(3, 1, rows_b)
        done(0, 1)
        a21p.wait_recv()
        a21m.wait_recv()
        to_sibling(2, 1, rows_a)
        zp.wait_recv()
        to_sibling(1, 1, rows_b)
        done(2, 0)
        done(3, 1)
        z2.wait_recv()
        to_sibling(2, 1, rows_b)
        done(1, 1)
        done(2, 1)
        yield

    own_pre.wait()
    for copy in pre_copies:
        copy.wait_recv()
    slope[...] = dot(preg[...].reshape(SHARDS * ROWS, UNITS), pt[...], 0, 0)

    def gelu(i, carry):
        rows = pl.ds(pl.multiple_of(i * 16, 16), 16)
        value, tilt = gelu_parts(slope[rows, :])
        act[gy, rows, :] = value.astype(BF16)
        slope[rows, :] = tilt
        return carry

    lax.fori_loop(0, UNITS // 16, gelu, 0)

    act_a = gather_a(act, HACT)
    act_b = gather_b(act, HACT)

    for copy in dy_last:
        copy.wait_recv()
    own_dy.wait()
    dyt[...] = compact(dyg, FEAT).astype(BF16)
    swap_dy = send(dyt, dys, C)
    x_first = ring_start(x_ref, xg, 1)
    load_wo.wait()
    swap_wo.wait_recv()

    ring = {}

    def ring_send(key, dy, dz, q0, q1, land):
        if dy == 2:
            ring[key, "relay+"] = send(part.at[dy, dz, q0], land.at[0], YP)
            ring[key, "relay-"] = send(part.at[dy, dz, q1], land.at[1], YM)
        if dy == 1:
            ring[key, "direct+"] = send(part.at[dy, dz, q1], land.at[2], YP)
        if dy == 3:
            ring[key, "direct-"] = send(part.at[dy, dz, q0], land.at[3], YM)

    def ring_pass(key, dz, q0, q1, land):
        ring[key, "relay+"].wait_recv()
        part[1, dz, q0, :] = (held[1, dz, q0, :] + land[0].astype(F32)).astype(BF16)
        ring[key, "last+"] = send(part.at[1, dz, q0], land.at[4], YP)
        ring[key, "relay-"].wait_recv()
        part[3, dz, q1, :] = (held[3, dz, q1, :] + land[1].astype(F32)).astype(BF16)
        ring[key, "last-"] = send(part.at[3, dz, q1], land.at[5], YM)

    def ring_total(key, dz, q0, q1, land):
        ring[key, "direct-"].wait_recv()
        ring[key, "last+"].wait_recv()
        total0 = held[0, dz, q0, :] + land[3].astype(F32) + land[4].astype(F32)
        ring[key, "direct+"].wait_recv()
        ring[key, "last-"].wait_recv()
        total1 = held[0, dz, q1, :] + land[2].astype(F32) + land[5].astype(F32)
        return total0, total1

    z_copies = {}
    for dy, dz in ((2, 1), (2, 0), (1, 1), (3, 1), (0, 1), (1, 0), (3, 0), (0, 0)):
        chip = ((y + dy) % 4) * 2 + (z + dz) % 2
        total = dot(wo_own[chip], dyt[...], 1, 0)
        if (dy, dz) == (2, 1):
            swap_dy.wait_recv()
        total = total + dot(wo_sib[chip], dys[...], 1, 0)
        held[dy, dz] = total
        part[dy, dz] = total.astype(BF16)
        ring_send(("a", dz), dy, dz, a0, a1, ry_a.at[dz])
        if dz == 1:
            z_copies[dy] = send(part.at[dy, dz, rows_b], rz_b.at[dy], Z)

    for dz in (1, 0):
        ring_pass(("a", dz), dz, a0, a1, ry_a.at[dz])
    x_last = ring_relay(xg, x_first)
    for dy in (2, 1, 3, 0):
        z_copies[dy].wait_recv()
        total = held[dy, 0, rows_b, :] + rz_b[dy].astype(F32)
        held[dy, 0, rows_b, :] = total
        part[dy, 0, rows_b, :] = total.astype(BF16)
        ring_send("b", dy, 0, b0, b1, ry_b)
        if dy == 3:
            ring_pass("b", 0, b0, b1, ry_b)
    total0, total1 = ring_total(("a", 1), 1, a0, a1, ry_a.at[1])
    part[0, 1, a0, :] = total0.astype(BF16)
    part[0, 1, a1, :] = total1.astype(BF16)
    z_last = send(part.at[0, 1, rows_a], rz_a, Z)

    def use_act(chip):
        block = act[pl.ds(chip * 2, 2)].reshape(2 * UNITS, LIVE)
        wo_out[chip] = dot(block, dyt[...], 1, 1).astype(BF16)

    act_steps = gather_rest(act, HACT, act_a, act_b, use_act)
    next(act_steps)

    total0, total1 = ring_total("b", 0, b0, b1, ry_b)
    hg[gy, b0, :] = (total0 * slope[b0, :]).astype(BF16)
    hg[gy, b1, :] = (total1 * slope[b1, :]).astype(BF16)
    hg_b = gather_b(hg, HA)
    total0, total1 = ring_total(("a", 0), 0, a0, a1, ry_a.at[0])
    z_last.wait_recv()
    hg[gy, a0, :] = ((total0 + rz_a[a0, :].astype(F32)) * slope[a0, :]).astype(BF16)
    hg[gy, a1, :] = ((total1 + rz_a[a1, :].astype(F32)) * slope[a1, :]).astype(BF16)
    hg_a = gather_a(hg, HA)

    next(act_steps)
    for copy in x_last:
        copy.wait_recv()
    own_x.wait()
    xt[...] = compact(xg, FEAT).astype(BF16)
    load_wi.wait()
    acc[...] = jnp.zeros_like(acc)

    late = []

    def block_of(buf, chip):
        return buf[pl.ds(chip * 2, 2)].reshape(2 * UNITS, LIVE)

    def use_hg(chip):
        columns = pl.ds(pl.multiple_of(chip * 2 * UNITS, 2 * UNITS), 2 * UNITS)
        block = block_of(hg, chip)
        acc[...] += dot(wi[:, columns], block, 1, 0)
        late.append(chip)
        if len(late) <= 4:
            wi_out[chip] = dot(xt[...], block, 1, 1).astype(BF16)

    hg_steps = gather_rest(hg, HA, hg_a, hg_b, use_hg)
    for _ in range(3):
        next(hg_steps)
    next(act_steps)
    next(hg_steps)

    half = FEAT // 2
    accb[...] = acc[...].astype(BF16)
    right_part[...] = dot(pt[...], accb[half:, :], 1, 1).astype(BF16).reshape(SHARDS, ROWS, half)
    far = pl.ds((1 - zh) * 4, 4)
    right_copy = send(right_part.at[far], right_z, ZH)
    left_part[...] = dot(pt[...], accb[:half, :], 1, 1).astype(BF16).reshape(SHARDS, ROWS, half)
    left_copies = [
        send(left_part.at[on_gx(d, dzh)], left_x.at[dzh, d - 1], (on_gx(d, 0), gy))
        for dzh in (1, 0) for d in (1, 2, 3)
    ]
    for chip in late[4:]:
        wi_out[chip] = dot(xt[...], block_of(hg, chip), 1, 1).astype(BF16)
    right_copy.wait_recv()
    right_last = []
    for d in (2, 1, 3):
        right_send[d - 1] = (
            right_part[on_gx(d, 0)].astype(F32) + right_z[(x + d) % 4].astype(F32)
        ).astype(BF16)
        right_last.append(send(right_send.at[d - 1], right_x.at[d - 1], (on_gx(d, 0), gy)))
    for copy in left_copies[:3]:
        copy.wait_recv()
    total = left_part[on_gx(0, 1)].astype(F32)
    for d in range(3):
        total = total + left_x[1, d].astype(F32)
    left_send[...] = total.astype(BF16)
    left_last = send(left_send, left_z, ZH)

    for _ in act_steps:
        pass

    for copy in left_copies[3:] + right_last + [left_last]:
        copy.wait_recv()
    total = left_part[gx].astype(F32) + left_z[...].astype(F32)
    for d in range(3):
        total = total + left_x[0, d].astype(F32)
    in_out[:, :half] = total.astype(BF16)
    total = right_part[gx].astype(F32) + right_z[x].astype(F32)
    for d in range(3):
        total = total + right_x[d].astype(F32)
    in_out[:, half:] = total.astype(BF16)
    for copy in sent:
        copy.wait_send()


def store_kernel(in_ref, wi_ref, wo_ref, in_out, wi_out, wo_out, sem):
    copies = [pltpu.make_async_copy(in_ref, in_out, sem.at[16])]
    for chip in range(8):
        span = pl.ds(chip * 2 * UNITS, 2 * UNITS)
        copies.append(pltpu.make_async_copy(wi_ref.at[chip], wi_out.at[:, span], sem.at[chip]))
        copies.append(pltpu.make_async_copy(wo_ref.at[chip], wo_out.at[span], sem.at[8 + chip]))
    for copy in copies:
        copy.start()
    for copy in copies:
        copy.wait()


def body(inputs, out_grad, pre_act, w_in, w_out, counts):
    vmem = pl.BlockSpec(memory_space=pltpu.VMEM)
    anywhere = pl.BlockSpec(memory_space=pl.ANY)
    qa, qb = HA // 2, HB // 2
    flops = 2 * 4 * LIVE * FEAT * UNITS * PIECES
    results = pl.pallas_call(
        kernel,
        out_shape=(
            pltpu.VMEM((ROWS, FEAT), BF16),
            pltpu.VMEM((8, FEAT, 2 * UNITS), BF16),
            pltpu.VMEM((8, 2 * UNITS, FEAT), BF16),
        ),
        in_specs=[pl.BlockSpec(memory_space=pltpu.SMEM)] + [anywhere] * 5,
        out_specs=(vmem, vmem, vmem),
        scratch_shapes=[
            pltpu.VMEM((SHARDS * ROWS, LIVE), BF16),
            pltpu.VMEM((SHARDS, ROWS, FEAT), BF16),
            pltpu.VMEM((SHARDS, ROWS, FEAT), BF16),
            pltpu.VMEM((PIECES, SHARDS * ROWS // PIECES, UNITS), BF16),
            pltpu.VMEM((FEAT, LIVE), BF16),
            pltpu.VMEM((FEAT, LIVE), BF16),
            pltpu.VMEM((FEAT, LIVE), BF16),
            pltpu.VMEM((8, UNITS, FEAT), BF16),
            pltpu.VMEM((8, UNITS, FEAT), BF16),
            pltpu.VMEM((FEAT, PIECES * UNITS), BF16),
            pltpu.VMEM((PIECES, UNITS, LIVE), BF16),
            pltpu.VMEM((PIECES, UNITS, LIVE), BF16),
            pltpu.VMEM((UNITS, LIVE), F32),
            pltpu.VMEM((4, 2, UNITS, LIVE), F32),
            pltpu.VMEM((4, 2, UNITS, LIVE), BF16),
            pltpu.VMEM((HA, LIVE), BF16),
            pltpu.VMEM((4, HB, LIVE), BF16),
            pltpu.VMEM((2, 6, qa, LIVE), BF16),
            pltpu.VMEM((6, qb, LIVE), BF16),
            pltpu.VMEM((FEAT, LIVE), F32),
            pltpu.VMEM((FEAT, LIVE), BF16),
            pltpu.VMEM((SHARDS, ROWS, FEAT // 2), BF16),
            pltpu.VMEM((SHARDS, ROWS, FEAT // 2), BF16),
            pltpu.VMEM((2, 3, ROWS, FEAT // 2), BF16),
            pltpu.VMEM((ROWS, FEAT // 2), BF16),
            pltpu.VMEM((ROWS, FEAT // 2), BF16),
            pltpu.VMEM((4, ROWS, FEAT // 2), BF16),
            pltpu.VMEM((3, ROWS, FEAT // 2), BF16),
            pltpu.VMEM((3, ROWS, FEAT // 2), BF16),
            pltpu.SemaphoreType.DMA((152,)),
            pltpu.SemaphoreType.DMA((152,)),
            pltpu.SemaphoreType.DMA((5,)),
        ],
        compiler_params=pltpu.CompilerParams(
            collective_id=0, has_side_effects=True, vmem_limit_bytes=48 * 1024 * 1024
        ),
        cost_estimate=pl.CostEstimate(flops=flops, bytes_accessed=16 << 20, transcendentals=UNITS * LIVE),
        name="ffn_backward",
    )(counts, inputs, out_grad, pre_act, w_in, w_out.reshape(8, 2, UNITS, FEAT))
    return pl.pallas_call(
        store_kernel,
        out_shape=(
            jax.ShapeDtypeStruct((ROWS, FEAT), BF16),
            jax.ShapeDtypeStruct((FEAT, PIECES * UNITS), BF16),
            jax.ShapeDtypeStruct((PIECES * UNITS, FEAT), BF16),
        ),
        in_specs=[vmem, vmem, vmem],
        out_specs=(anywhere, anywhere, anywhere),
        scratch_shapes=[pltpu.SemaphoreType.DMA((17,))],
        compiler_params=pltpu.CompilerParams(vmem_limit_bytes=16 * 1024 * 1024),
        name="store_results",
    )(*results)


def solution(mesh):
    return jax.shard_map(
        body,
        mesh=mesh,
        in_specs=(P("gx", "gy"), P("gx", "gy"), P("gy", "gx"), P("gy", "gx"), P("gx", "gy"), P()),
        out_specs=(P("gx", "gy"), P("gy", "gx"), P("gx", "gy")),
        check_vma=False,
    )
```

```python
import math

import jax
import jax.numpy as jnp
from jax import lax
from jax.experimental import pallas as pl
from jax.experimental.pallas import tpu as pltpu
from jax.sharding import PartitionSpec as P

LIVE = 640
SHARDS = 8
ROWS = 128
FEAT = 512
PIECES = 16
UNITS = 256
HA = 160
HACT = 192
HB = UNITS - HA
MESH = pl.DeviceIdType.MESH
BF16, F32 = jnp.bfloat16, jnp.float32

gelu_scale = math.sqrt(2.0 / math.pi)
cubic_coef = 0.044715


def gelu_parts(pre):
    tangent = jnp.tanh(gelu_scale * (pre + cubic_coef * pre * pre * pre))
    value = 0.5 * pre * (1.0 + tangent)
    slope = 0.5 * (1.0 + tangent) + 0.5 * pre * (1.0 - tangent * tangent) * gelu_scale * (
        1.0 + 3.0 * cubic_coef * pre * pre
    )
    return value, slope


def dot(left, right, left_dim, right_dim):
    return lax.dot_general(
        left, right, (((left_dim,), (right_dim,)), ((), ())), preferred_element_type=F32
    )


def kernel(
    counts, x_ref, dy_ref, pre_ref, w_in_ref, w_out_ref,
    in_out, wi_out, wo_out,
    pt, dyg, xg, preg, dyt, dys, xt, wo_own, wo_sib, wi, act, hg, slope,
    held, part, rz_a, rz_b, ry_a, ry_b, acc, accb, left_part, right_part, left_x, left_send, left_z, right_z, right_send, right_x,
    send_sem, recv_sem, local_sem,
):
    gx, gy = lax.axis_index("gx"), lax.axis_index("gy")
    x, zh = gx % 4, gx // 4
    core, z, y = gy % 2, (gy // 2) % 2, gy // 4

    def on_gy(dy, dz, dc=0):
        return ((y + dy) % 4) * 4 + ((z + dz) % 2) * 2 + (core + dc) % 2

    def on_gx(dx, dzh):
        return ((zh + dzh) % 2) * 4 + (x + dx) % 4

    YP, YM, Z, C = (gx, on_gy(1, 0)), (gx, on_gy(3, 0)), (gx, on_gy(0, 1)), (gx, on_gy(0, 0, 1))
    XP, XM, ZH = (on_gx(1, 0), gy), (on_gx(3, 0), gy), (on_gx(0, 1), gy)

    count = [0, 0]
    sent = []

    def send(src, dst, device):
        k = count[0]
        count[0] += 1
        copy = pltpu.make_async_remote_copy(
            src_ref=src, dst_ref=dst, send_sem=send_sem.at[k], recv_sem=recv_sem.at[k],
            device_id=device, device_id_type=MESH,
        )
        copy.start()
        sent.append(copy)
        return copy

    def local(src, dst):
        k = count[1]
        count[1] += 1
        copy = pltpu.make_async_copy(src, dst, local_sem.at[k])
        copy.start()
        return copy

    own_pre = local(pre_ref.at[:, pl.ds(pl.multiple_of(gy * UNITS, UNITS), UNITS)], preg.at[gy])
    own_dy, own_x = local(dy_ref, dyg.at[gx]), local(x_ref, xg.at[gx])
    load_wo = local(w_out_ref.at[:, core], wo_own)
    load_wi = local(w_in_ref, wi)
    barrier = pltpu.get_barrier_semaphore()
    for d in range(1, PIECES):
        pl.semaphore_signal(barrier, inc=1, device_id=(gx, (gy + d) % PIECES), device_id_type=MESH)
    for d in range(1, SHARDS):
        pl.semaphore_signal(barrier, inc=1, device_id=((gx + d) % SHARDS, gy), device_id_type=MESH)

    pl.semaphore_wait(barrier, PIECES - 1 + SHARDS - 1)

    def ring_start(src, buf, chunks):
        size = ROWS // chunks
        return [
            [send(src.at[pl.ds(k * size, size)], buf.at[gx, pl.ds(k * size, size)], to) for to in (ZH, XP, XM)]
            for k in range(chunks)
        ]

    def ring_relay(buf, first):
        size = ROWS // len(first)
        last, second = [], []

        def pass_on(k, dzh, to_right, to_left):
            to_right.wait_recv()
            piece = buf.at[on_gx(3, dzh), pl.ds(k * size, size // 2)]
            last.append(send(piece, piece, XP))
            to_left.wait_recv()
            piece = buf.at[on_gx(1, dzh), pl.ds(k * size + size // 2, size // 2)]
            last.append(send(piece, piece, XM))

        for k, (across, right, left) in enumerate(first):
            across.wait_recv()
            piece = buf.at[on_gx(0, 1), pl.ds(k * size, size)]
            second.append((send(piece, piece, XP), send(piece, piece, XM)))
            pass_on(k, 0, right, left)
        for k, (right, left) in enumerate(second):
            pass_on(k, 1, right, left)
        return last

    dy_first = ring_start(dy_ref, dyg, 2)
    pre_copies = []
    for d in range(1, PIECES):
        to = (gy + d) % PIECES
        columns = pl.ds(pl.multiple_of(to * UNITS, UNITS), UNITS)
        pre_copies.append(send(pre_ref.at[:, columns], preg.at[gy], (gx, to)))
    swap_wo = send(w_out_ref.at[:, 1 - core], wo_sib, C)
    start = jnp.int32(0)
    for s in range(SHARDS):
        number = counts[s]

        def fill(i, carry, s=s, start=start, number=number):
            slot = lax.broadcasted_iota(jnp.int32, (16, LIVE), 0) + i * 16
            column = lax.broadcasted_iota(jnp.int32, (16, LIVE), 1)
            hit = (column == slot + start) & (slot < number)
            pt[pl.ds(pl.multiple_of(s * ROWS + i * 16, 16), 16), :] = jnp.where(hit, 1.0, 0.0).astype(BF16)
            return carry

        lax.fori_loop(0, ROWS // 16, fill, 0)
        start = start + number
    dy_last = ring_relay(dyg, dy_first)

    def compact(buf, width):
        whole = buf[...].reshape(SHARDS * ROWS, width)
        return dot(whole, pt[...], 0, 0)

    def split(ha):
        qa, qb = ha // 2, (UNITS - ha) // 2
        return (
            pl.ds(0, ha), pl.ds(ha, 2 * qb), pl.ds(0, qa), pl.ds(qa, qa), pl.ds(ha, qb), pl.ds(ha + qb, qb)
        )

    rows_a, rows_b, a0, a1, b0, b1 = split(HA)

    def gather_a(buf, ha):
        rows_a = split(ha)[0]
        own = buf.at[gy, rows_a]
        return {"z": send(own, own, Z), "+": send(own, own, YP), "-": send(own, own, YM), "c": send(own, own, C)}

    def gather_b(buf, ha):
        rows_b = split(ha)[1]
        own = buf.at[gy, rows_b]
        return {"+": send(own, own, YP), "-": send(own, own, YM), "z": send(own, own, Z), "c": send(own, own, C)}

    def gather_rest(buf, ha, fa, fb, use):
        rows_a, rows_b, a0, a1, b0, b1 = split(ha)
        sib = {(0, 0): [fa["c"], fb["c"]]}

        def fwd(dy, dz, rows, device):
            piece = buf.at[on_gy(dy, dz), rows]
            return send(piece, piece, device)

        def to_sibling(dy, dz, rows):
            sib.setdefault((dy, dz), []).append(fwd(dy, dz, rows, C))

        def done(dy, dz):
            for copy in sib[dy, dz]:
                copy.wait_recv()
            use(((y + dy) % 4) * 2 + (z + dz) % 2)

        fa["z"].wait_recv()
        plus = fwd(0, 1, rows_a, YP)
        minus = fwd(0, 1, rows_a, YM)
        to_sibling(0, 1, rows_a)
        fa["+"].wait_recv()
        a20p = fwd(3, 0, a0, YP)
        to_sibling(3, 0, rows_a)
        fa["-"].wait_recv()
        a20m = fwd(1, 0, a1, YM)
        to_sibling(1, 0, rows_a)
        fb["+"].wait_recv()
        b20p = fwd(3, 0, b0, YP)
        zm = fwd(3, 0, rows_b, Z)
        to_sibling(3, 0, rows_b)
        fb["-"].wait_recv()
        b20m = fwd(1, 0, b1, YM)
        zp = fwd(1, 0, rows_b, Z)
        to_sibling(1, 0, rows_b)
        yield
        done(0, 0)
        yield
        plus.wait_recv()
        a21p = fwd(3, 1, a0, YP)
        to_sibling(3, 1, rows_a)
        minus.wait_recv()
        a21m = fwd(1, 1, a1, YM)
        to_sibling(1, 1, rows_a)
        a20p.wait_recv()
        a20m.wait_recv()
        to_sibling(2, 0, rows_a)
        b20p.wait_recv()
        b20m.wait_recv()
        z2 = fwd(2, 0, rows_b, Z)
        to_sibling(2, 0, rows_b)
        fb["z"].wait_recv()
        to_sibling(0, 1, rows_b)
        done(3, 0)
        done(1, 0)
        yield
        zm.wait_recv()
        to_sibling(3, 1, rows_b)
        done(0, 1)
        a21p.wait_recv()
        a21m.wait_recv()
        to_sibling(2, 1, rows_a)
        zp.wait_recv()
        to_sibling(1, 1, rows_b)
        done(2, 0)
        done(3, 1)
        z2.wait_recv()
        to_sibling(2, 1, rows_b)
        done(1, 1)
        done(2, 1)
        yield

    own_pre.wait()
    for copy in pre_copies:
        copy.wait_recv()
    slope[...] = dot(preg[...].reshape(SHARDS * ROWS, UNITS), pt[...], 0, 0)

    def gelu(i, carry):
        rows = pl.ds(pl.multiple_of(i * 16, 16), 16)
        value, tilt = gelu_parts(slope[rows, :])
        act[gy, rows, :] = value.astype(BF16)
        slope[rows, :] = tilt
        return carry

    lax.fori_loop(0, UNITS // 16, gelu, 0)

    act_a = gather_a(act, HACT)
    act_b = gather_b(act, HACT)

    for copy in dy_last:
        copy.wait_recv()
    own_dy.wait()
    dyt[...] = compact(dyg, FEAT).astype(BF16)
    swap_dy = send(dyt, dys, C)
    x_first = ring_start(x_ref, xg, 1)
    load_wo.wait()
    swap_wo.wait_recv()

    ring = {}

    def ring_send(key, dy, dz, q0, q1, land):
        if dy == 2:
            ring[key, "relay+"] = send(part.at[dy, dz, q0], land.at[0], YP)
            ring[key, "relay-"] = send(part.at[dy, dz, q1], land.at[1], YM)
        if dy == 1:
            ring[key, "direct+"] = send(part.at[dy, dz, q1], land.at[2], YP)
        if dy == 3:
            ring[key, "direct-"] = send(part.at[dy, dz, q0], land.at[3], YM)

    def ring_pass(key, dz, q0, q1, land):
        ring[key, "relay+"].wait_recv()
        part[1, dz, q0, :] = (held[1, dz, q0, :] + land[0].astype(F32)).astype(BF16)
        ring[key, "last+"] = send(part.at[1, dz, q0], land.at[4], YP)
        ring[key, "relay-"].wait_recv()
        part[3, dz, q1, :] = (held[3, dz, q1, :] + land[1].astype(F32)).astype(BF16)
        ring[key, "last-"] = send(part.at[3, dz, q1], land.at[5], YM)

    def ring_total(key, dz, q0, q1, land):
        ring[key, "direct-"].wait_recv()
        ring[key, "last+"].wait_recv()
        total0 = held[0, dz, q0, :] + land[3].astype(F32) + land[4].astype(F32)
        ring[key, "direct+"].wait_recv()
        ring[key, "last-"].wait_recv()
        total1 = held[0, dz, q1, :] + land[2].astype(F32) + land[5].astype(F32)
        return total0, total1

    z_copies = {}
    for dy, dz in ((2, 1), (2, 0), (1, 1), (3, 1), (0, 1), (1, 0), (3, 0), (0, 0)):
        chip = ((y + dy) % 4) * 2 + (z + dz) % 2
        total = dot(wo_own[chip], dyt[...], 1, 0)
        if (dy, dz) == (2, 1):
            swap_dy.wait_recv()
        total = total + dot(wo_sib[chip], dys[...], 1, 0)
        held[dy, dz] = total
        part[dy, dz] = total.astype(BF16)
        ring_send(("a", dz), dy, dz, a0, a1, ry_a.at[dz])
        if dz == 1:
            z_copies[dy] = send(part.at[dy, dz, rows_b], rz_b.at[dy], Z)

    for dz in (1, 0):
        ring_pass(("a", dz), dz, a0, a1, ry_a.at[dz])
    for dy in (2, 1, 3, 0):
        z_copies[dy].wait_recv()
        total = held[dy, 0, rows_b, :] + rz_b[dy].astype(F32)
        held[dy, 0, rows_b, :] = total
        part[dy, 0, rows_b, :] = total.astype(BF16)
        ring_send("b", dy, 0, b0, b1, ry_b)
        if dy == 3:
            ring_pass("b", 0, b0, b1, ry_b)
    x_last = ring_relay(xg, x_first)
    total0, total1 = ring_total(("a", 1), 1, a0, a1, ry_a.at[1])
    part[0, 1, a0, :] = total0.astype(BF16)
    part[0, 1, a1, :] = total1.astype(BF16)
    z_last = send(part.at[0, 1, rows_a], rz_a, Z)

    def use_act(chip):
        block = act[pl.ds(chip * 2, 2)].reshape(2 * UNITS, LIVE)
        wo_out[chip] = dot(block, dyt[...], 1, 1).astype(BF16)

    act_steps = gather_rest(act, HACT, act_a, act_b, use_act)
    next(act_steps)

    total0, total1 = ring_total("b", 0, b0, b1, ry_b)
    hg[gy, b0, :] = (total0 * slope[b0, :]).astype(BF16)
    hg[gy, b1, :] = (total1 * slope[b1, :]).astype(BF16)
    hg_b = gather_b(hg, HA)
    total0, total1 = ring_total(("a", 0), 0, a0, a1, ry_a.at[0])
    z_last.wait_recv()
    hg[gy, a0, :] = ((total0 + rz_a[a0, :].astype(F32)) * slope[a0, :]).astype(BF16)
    hg[gy, a1, :] = ((total1 + rz_a[a1, :].astype(F32)) * slope[a1, :]).astype(BF16)
    hg_a = gather_a(hg, HA)

    next(act_steps)
    for copy in x_last:
        copy.wait_recv()
    own_x.wait()
    xt[...] = compact(xg, FEAT).astype(BF16)
    load_wi.wait()
    acc[...] = jnp.zeros_like(acc)

    late = []

    def block_of(buf, chip):
        return buf[pl.ds(chip * 2, 2)].reshape(2 * UNITS, LIVE)

    def use_hg(chip):
        columns = pl.ds(pl.multiple_of(chip * 2 * UNITS, 2 * UNITS), 2 * UNITS)
        block = block_of(hg, chip)
        acc[...] += dot(wi[:, columns], block, 1, 0)
        late.append(chip)
        if len(late) <= 4:
            wi_out[chip] = dot(xt[...], block, 1, 1).astype(BF16)

    hg_steps = gather_rest(hg, HA, hg_a, hg_b, use_hg)
    for _ in range(3):
        next(hg_steps)
    next(act_steps)
    next(hg_steps)

    half = FEAT // 2
    accb[...] = acc[...].astype(BF16)
    right_part[...] = dot(pt[...], accb[half:, :], 1, 1).astype(BF16).reshape(SHARDS, ROWS, half)
    far = pl.ds((1 - zh) * 4, 4)
    right_copy = send(right_part.at[far], right_z, ZH)
    left_part[...] = dot(pt[...], accb[:half, :], 1, 1).astype(BF16).reshape(SHARDS, ROWS, half)
    left_copies = [
        send(left_part.at[on_gx(d, dzh)], left_x.at[dzh, d - 1], (on_gx(d, 0), gy))
        for dzh in (1, 0) for d in (1, 2, 3)
    ]
    for chip in late[4:]:
        wi_out[chip] = dot(xt[...], block_of(hg, chip), 1, 1).astype(BF16)
    right_copy.wait_recv()
    right_last = []
    for d in (2, 1, 3):
        right_send[d - 1] = (
            right_part[on_gx(d, 0)].astype(F32) + right_z[(x + d) % 4].astype(F32)
        ).astype(BF16)
        right_last.append(send(right_send.at[d - 1], right_x.at[d - 1], (on_gx(d, 0), gy)))
    for copy in left_copies[:3]:
        copy.wait_recv()
    total = left_part[on_gx(0, 1)].astype(F32)
    for d in range(3):
        total = total + left_x[1, d].astype(F32)
    left_send[...] = total.astype(BF16)
    left_last = send(left_send, left_z, ZH)

    for _ in act_steps:
        pass

    for copy in left_copies[3:] + right_last + [left_last]:
        copy.wait_recv()
    total = left_part[gx].astype(F32) + left_z[...].astype(F32)
    for d in range(3):
        total = total + left_x[0, d].astype(F32)
    in_out[:, :half] = total.astype(BF16)
    total = right_part[gx].astype(F32) + right_z[x].astype(F32)
    for d in range(3):
        total = total + right_x[d].astype(F32)
    in_out[:, half:] = total.astype(BF16)
    for copy in sent:
        copy.wait_send()


def store_kernel(in_ref, wi_ref, wo_ref, in_out, wi_out, wo_out, sem):
    copies = [pltpu.make_async_copy(in_ref, in_out, sem.at[16])]
    for chip in range(8):
        span = pl.ds(chip * 2 * UNITS, 2 * UNITS)
        copies.append(pltpu.make_async_copy(wi_ref.at[chip], wi_out.at[:, span], sem.at[chip]))
        copies.append(pltpu.make_async_copy(wo_ref.at[chip], wo_out.at[span], sem.at[8 + chip]))
    for copy in copies:
        copy.start()
    for copy in copies:
        copy.wait()


def body(inputs, out_grad, pre_act, w_in, w_out, counts):
    vmem = pl.BlockSpec(memory_space=pltpu.VMEM)
    anywhere = pl.BlockSpec(memory_space=pl.ANY)
    qa, qb = HA // 2, HB // 2
    flops = 2 * 4 * LIVE * FEAT * UNITS * PIECES
    results = pl.pallas_call(
        kernel,
        out_shape=(
            pltpu.VMEM((ROWS, FEAT), BF16),
            pltpu.VMEM((8, FEAT, 2 * UNITS), BF16),
            pltpu.VMEM((8, 2 * UNITS, FEAT), BF16),
        ),
        in_specs=[pl.BlockSpec(memory_space=pltpu.SMEM)] + [anywhere] * 5,
        out_specs=(vmem, vmem, vmem),
        scratch_shapes=[
            pltpu.VMEM((SHARDS * ROWS, LIVE), BF16),
            pltpu.VMEM((SHARDS, ROWS, FEAT), BF16),
            pltpu.VMEM((SHARDS, ROWS, FEAT), BF16),
            pltpu.VMEM((PIECES, SHARDS * ROWS // PIECES, UNITS), BF16),
            pltpu.VMEM((FEAT, LIVE), BF16),
            pltpu.VMEM((FEAT, LIVE), BF16),
            pltpu.VMEM((FEAT, LIVE), BF16),
            pltpu.VMEM((8, UNITS, FEAT), BF16),
            pltpu.VMEM((8, UNITS, FEAT), BF16),
            pltpu.VMEM((FEAT, PIECES * UNITS), BF16),
            pltpu.VMEM((PIECES, UNITS, LIVE), BF16),
            pltpu.VMEM((PIECES, UNITS, LIVE), BF16),
            pltpu.VMEM((UNITS, LIVE), F32),
            pltpu.VMEM((4, 2, UNITS, LIVE), F32),
            pltpu.VMEM((4, 2, UNITS, LIVE), BF16),
            pltpu.VMEM((HA, LIVE), BF16),
            pltpu.VMEM((4, HB, LIVE), BF16),
            pltpu.VMEM((2, 6, qa, LIVE), BF16),
            pltpu.VMEM((6, qb, LIVE), BF16),
            pltpu.VMEM((FEAT, LIVE), F32),
            pltpu.VMEM((FEAT, LIVE), BF16),
            pltpu.VMEM((SHARDS, ROWS, FEAT // 2), BF16),
            pltpu.VMEM((SHARDS, ROWS, FEAT // 2), BF16),
            pltpu.VMEM((2, 3, ROWS, FEAT // 2), BF16),
            pltpu.VMEM((ROWS, FEAT // 2), BF16),
            pltpu.VMEM((ROWS, FEAT // 2), BF16),
            pltpu.VMEM((4, ROWS, FEAT // 2), BF16),
            pltpu.VMEM((3, ROWS, FEAT // 2), BF16),
            pltpu.VMEM((3, ROWS, FEAT // 2), BF16),
            pltpu.SemaphoreType.DMA((152,)),
            pltpu.SemaphoreType.DMA((152,)),
            pltpu.SemaphoreType.DMA((5,)),
        ],
        compiler_params=pltpu.CompilerParams(
            collective_id=0, has_side_effects=True, vmem_limit_bytes=48 * 1024 * 1024
        ),
        cost_estimate=pl.CostEstimate(flops=flops, bytes_accessed=16 << 20, transcendentals=UNITS * LIVE),
        name="ffn_backward",
    )(counts, inputs, out_grad, pre_act, w_in, w_out.reshape(8, 2, UNITS, FEAT))
    return pl.pallas_call(
        store_kernel,
        out_shape=(
            jax.ShapeDtypeStruct((ROWS, FEAT), BF16),
            jax.ShapeDtypeStruct((FEAT, PIECES * UNITS), BF16),
            jax.ShapeDtypeStruct((PIECES * UNITS, FEAT), BF16),
        ),
        in_specs=[vmem, vmem, vmem],
        out_specs=(anywhere, anywhere, anywhere),
        scratch_shapes=[pltpu.SemaphoreType.DMA((17,))],
        compiler_params=pltpu.CompilerParams(vmem_limit_bytes=16 * 1024 * 1024),
        name="store_results",
    )(*results)


def solution(mesh):
    return jax.shard_map(
        body,
        mesh=mesh,
        in_specs=(P("gx", "gy"), P("gx", "gy"), P("gy", "gx"), P("gy", "gx"), P("gx", "gy"), P()),
        out_specs=(P("gx", "gy"), P("gy", "gx"), P("gx", "gy")),
        check_vma=False,
    )
```
